256 devices in a mesh: grp: 2 (over z_lo), head: 4 (over x), seq: 32 (over y, z_hi, core).
Axes of the slice: x: 4, y: 4, z: 8 (z_hi: 4, z_lo: 2; z = z_hi * 2 + z_lo), core: 2. Of those that a mesh axis runs over, the one named last changes fastest.
Arguments:
- queries: bfloat16 [64, 4096, 128], P('head', 'seq'), may hold values from -6 to 6
- keys: bfloat16 [4, 4096, 128], P('head', 'seq'), may hold values from -6 to 6
- values: bfloat16 [4, 4096, 128], P('head', 'seq'), may hold values from -6 to 6
- feature_map: bfloat16 [64, 128, 128], P('head'), may hold values from -0.5 to 0.5
Outputs:
- feature_grad: float32 [64, 128, 128], P('head', ('grp', 'seq'))
The draws below stay inside these ranges and needn't reach their ends.
All inputs are finite; a program needn't handle non-finite values.
Results may differ from the reference program's by a relative error of at most 0.0044.
Values may be sent and summed in bfloat16 or wider, within the bound.
A program may use at most 128 MiB of HBM per device.

```python
import jax
import jax.numpy as jnp
from jax import lax

DH = 128
GROUP = 16
FEAT = 128
KVH = 4
HEADS = 64
TOKENS = 4096


def level_of(key, shape, shards, least, largest):
    def one(position, shards_of):
        steps = jax.random.uniform(jax.random.fold_in(jax.random.fold_in(key, 6), position), (shards_of,), jnp.float32, least / len(shards), largest / len(shards))
        return jnp.repeat(jnp.exp(steps), shape[position] // shards_of).reshape((-1,) + (1,) * (len(shape) - position - 1))

    loudness = one(*shards[0])
    for cut in shards[1:]:
        loudness = loudness * one(*cut)
    return loudness


def normal_values(key, dims, deviation, bound, cuts=(), kind=jnp.bfloat16):
    factor_of = level_of(key, dims, cuts, -0.22, 0.18) if cuts else 1.0
    drawn = jax.random.normal(key, dims, jnp.float32) * deviation * factor_of
    return jnp.minimum(jnp.maximum(drawn, -bound), bound).astype(kind)


def setup_inputs(seed: int = 0) -> dict:
    key_list = jax.random.split(jax.random.key(seed), 5)
    return {
        "queries": normal_values(key_list[0], (HEADS, TOKENS, DH), 1.0, 6.0, ((0, 4), (1, 32))),
        "keys": normal_values(key_list[1], (KVH, TOKENS, DH), 1.0, 6.0, ((0, 4), (1, 32))),
        "values": normal_values(key_list[2], (KVH, TOKENS, DH), 1.0, 6.0, ((0, 4), (1, 32))),
        "feature_map": normal_values(key_list[3], (HEADS, DH, FEAT), DH ** -0.5, 0.5, ((0, 4),)),
    }


def teacher_head(queries, keys, values, index):
    kv_index = index // GROUP
    query_rows = queries[index]
    key_rows = keys[kv_index]
    value_rows = values[kv_index]
    scores = jnp.dot(query_rows, key_rows.T, preferred_element_type=jnp.float32) / jnp.sqrt(jnp.float32(DH))
    causal = jnp.tril(jnp.ones((TOKENS, TOKENS), dtype=bool))
    weights = jnp.where(causal, jnp.exp(scores), jnp.float32(0.0))
    denom = lax.optimization_barrier(jnp.sum(weights, axis=1))
    numer = jnp.dot(weights.astype(jnp.bfloat16), value_rows, preferred_element_type=jnp.float32)
    return (numer / denom[:, None]).astype(jnp.bfloat16)

def student_head(query_rows, key_rows, value_rows, wmat):
    hp = lax.Precision.HIGHEST
    phi_q = jnp.exp(jnp.dot(query_rows, wmat, precision=hp))
    phi_k = jnp.exp(jnp.dot(key_rows, wmat, precision=hp))
    causal = jnp.tril(jnp.ones((TOKENS, TOKENS), dtype=jnp.float32))
    scores = jnp.dot(phi_q, phi_k.T, precision=hp) * causal
    numer = jnp.dot(scores, value_rows, precision=hp)
    denom = lax.optimization_barrier(jnp.sum(scores, axis=1))
    return numer / denom[:, None]

def reference(queries, keys, values, feature_map):
    indices = jnp.arange(HEADS, dtype=jnp.int32)
    teacher = lax.map(lambda idx: teacher_head(queries, keys, values, idx), indices)
    target = teacher.astype(jnp.float32)
    query_f = queries.astype(jnp.float32)
    key_f = keys.astype(jnp.float32)
    value_f = values.astype(jnp.float32)

    def loss_of(weights):

        def one_head(index):
            kv_index = index // GROUP
            student = student_head(query_f[index], key_f[kv_index], value_f[kv_index], weights[index])
            return jnp.sum((student - target[index]) ** 2)
        return jnp.sum(lax.map(one_head, indices)) / jnp.float32(TOKENS)
    return jax.grad(loss_of)(feature_map.astype(jnp.float32))
```

```python
import functools
import math

import jax
import jax.numpy as jnp
from jax import lax
from jax.experimental import pallas as pl
from jax.experimental.pallas import tpu as pltpu
from jax.sharding import PartitionSpec as P

MESH = pl.DeviceIdType.MESH
F32 = jnp.float32
BF16 = jnp.bfloat16
BLOCK = 128
CHUNK = 256
D = 128
YS, PAIRS, CORES, GRPS = 4, 4, 2, 2
LAST = (((1,), (1,)), ((), ()))
PLAIN = (((1,), (0,)), ((), ()))


def dot(a, b, dims=PLAIN):
    return lax.dot_general(a, b, dims, preferred_element_type=F32)


def split(x):
    hi = x.astype(BF16)
    return hi, (x - hi.astype(F32)).astype(BF16)


def dot2(a, b, dims=PLAIN):
    return dot(a[0], b, dims) + dot(a[1], b, dims)


def dot3(a, b, dims=PLAIN):
    return dot(a[0], b[0], dims) + (dot(a[0], b[1], dims) + dot(a[1], b[0], dims))


def kernel(
    tokens,
    q_ref,
    k_ref,
    v_ref,
    fm_ref,
    out_ref,
    qbuf,
    kv,
    wbuf,
    phik,
    phiq,
    phiqt,
    intra,
    numer,
    denom,
    state_all,
    state_own,
    cot,
    dphik_own,
    f1_out,
    f1_in,
    f2_out,
    f2_in,
    loc_sem,
    q_send,
    q_recv,
    col_send,
    col_recv,
    right_send,
    right_recv,
    left_send,
    left_recv,
    sib_send,
    sib_recv,
    f1_send,
    f1_recv,
    f2_send,
    f2_recv,
):
    g = lax.axis_index("grp")
    s = lax.axis_index("seq")
    y = lax.div(s, 8)
    zh = lax.rem(lax.div(s, 2), 4)
    c = lax.rem(s, 2)
    z = 2 * zh + g
    head = y * 4 + g * 2 + c

    def seq_of(yy, hh, cc):
        return yy * 8 + hh * 2 + cc

    def device(yy, zz, cc):
        return {"grp": lax.rem(zz, 2), "seq": seq_of(yy, lax.div(zz, 2), cc)}

    def at(zz, yy, cc):
        return kv.at[lax.rem(zz, 2), lax.div(zz, 2), yy, cc]

    def column(zz, cc):
        return kv.at[lax.rem(zz, 2), lax.div(zz, 2), :, cc]

    def remote(src, dst, send, recv, dev):
        return pltpu.make_async_remote_copy(
            src_ref=src, dst_ref=dst, send_sem=send, recv_sem=recv,
            device_id=dev, device_id_type=MESH,
        )

    own = at(z, y, c)

    @pl.when(g == 0)
    def _():
        pltpu.make_async_copy(k_ref.at[0], own, loc_sem.at[0]).start()

    @pl.when(g == 1)
    def _():
        pltpu.make_async_copy(v_ref.at[0], own, loc_sem.at[0]).start()

    copy_q = pltpu.make_async_copy(q_ref.at[head], qbuf.at[y, c], loc_sem.at[1])
    copy_q.start()
    copy_w = pltpu.make_async_copy(fm_ref.at[head], wbuf, loc_sem.at[2])
    copy_w.start()

    other_y = lambda d: lax.rem(y + d, 4)
    other_z = lambda d: lax.rem(z + d, 8)
    other_c = lambda d: lax.rem(c + d, 2)
    group = [
        (dy, dg, dc)
        for dy in range(YS) for dg in range(GRPS) for dc in range(CORES)
        if (dy, dg, dc) != (0, 0, 0)
    ]
    z_pair = lambda d: 2 * zh + lax.rem(g + d, 2)
    next_z, prev_z = other_z(1), other_z(7)
    outer_z = lax.rem(z + 8 + 2 * g - 1, 8)

    barrier = pltpu.get_barrier_semaphore()
    partners = [device(other_y(dy), z_pair(dg), other_c(dc)) for dy, dg, dc in group]
    partners += [device(y, other_z(2 * d), c) for d in (1, 2, 3)]
    partners += [device(y, outer_z, c)]
    for dev in partners:
        pl.semaphore_signal(barrier, inc=1, device_id=dev, device_id_type=MESH)
    pltpu.make_async_copy(k_ref.at[0], own, loc_sem.at[0]).wait()
    pl.semaphore_wait(barrier, len(partners))

    sent = []

    def send(*args):
        copy = remote(*args)
        copy.start()
        sent.append(copy)

    rows = [y, other_y(3), other_y(1), other_y(2)]
    step_of = [0, 1, 3, 2]

    def ring(hop, i):
        if hop < 4 or i < 2:
            ref = at(other_z(8 - (hop - 1)), rows[i], c)
            send(ref, ref, right_send.at[hop - 1, i], right_recv.at[hop - 1, i], device(y, next_z, c))
        if hop < 4 or i >= 2:
            ref = at(other_z(hop - 1), rows[i], c)
            send(ref, ref, left_send.at[hop - 1, i], left_recv.at[hop - 1, i], device(y, prev_z, c))

    def arrived(hop, i):
        if hop < 4 or i < 2:
            ref = at(other_z(8 - hop), rows[i], c)
            remote(ref, ref, right_send.at[hop - 1, i], right_recv.at[hop - 1, i], device(y, prev_z, c)).wait_recv()
        if hop < 4 or i >= 2:
            ref = at(other_z(hop), rows[i], c)
            remote(ref, ref, left_send.at[hop - 1, i], left_recv.at[hop - 1, i], device(y, next_z, c)).wait_recv()

    def sibling(j, offset):
        ref = column(other_z(offset), c)
        send(ref, ref, sib_send.at[j], sib_recv.at[j], device(y, z, other_c(1)))

    def from_sibling(j, offset):
        ref = column(other_z(offset), other_c(1))
        remote(ref, ref, sib_send.at[j], sib_recv.at[j], device(y, z, other_c(1))).wait_recv()

    for i in (1, 2, 3):
        d = step_of[i]
        send(own, own, col_send.at[d], col_recv.at[d], device(other_y(d), z, c))
    ring(1, 0)
    for dy in (1, 3, 2, 0):
        for dc in (0, 1):
            if dy == 0 and dc == 0:
                continue
            to_head = other_y(dy) * 4 + g * 2 + other_c(dc)
            j = dy * 2 + dc
            send(
                q_ref.at[to_head], qbuf.at[y, c], q_send.at[j], q_recv.at[j],
                device(other_y(dy), z, other_c(dc)),
            )

    copy_w.wait()
    w = wbuf[...]
    wt = w.astype(F32).T.astype(BF16)
    ones = jnp.ones((CHUNK, D), BF16)
    row_id = lax.broadcasted_iota(jnp.int32, (CHUNK, CHUNK), 0)
    col_id = lax.broadcasted_iota(jnp.int32, (CHUNK, CHUNK), 1)
    causal = col_id <= row_id
    scale = math.log2(math.e) / math.sqrt(D)

    def query(yq):
        return qbuf[yq].reshape(CHUNK, D)

    def key(pair, yk):
        return kv[0, pair, yk].reshape(CHUNK, D)

    def value(pair, yk):
        return kv[1, pair, yk].reshape(CHUNK, D)

    def value_one(pair, yk):
        return jnp.concatenate([value(pair, yk), ones], axis=1)

    def attend(pair, yq, first, count, masked, new):
        n = count * CHUNK
        keys = kv[0, pair, pl.ds(first, count)].reshape(n, D)
        vals = kv[1, pair, pl.ds(first, count)].reshape(n, D)
        p = jnp.exp2(dot(query(yq), keys, LAST) * scale)
        if masked:
            p = jnp.where(causal, p, 0.0)
        part = sum(p[:, k * D : (k + 1) * D] for k in range(n // D))
        out = dot(p.astype(BF16), vals)
        if new:
            denom[yq] = part
            numer[yq] = out
        else:
            denom[yq] += part
            numer[yq] += out

    def teacher(pair, is_own):
        for yq in range(YS):
            if is_own:
                attend(pair, yq, yq, 1, True, True)
            if yq > 0:
                attend(pair, yq, 0, yq, False, False)
        if not is_own:

            @pl.when(pair < zh)
            def _():
                for yq in range(YS):
                    attend(pair, yq, yq, 1, False, False)

    def student_keys(pair, is_own):
        ks = kv[0, pair].reshape(YS * CHUNK, D)
        phi = jnp.exp(dot(wt, ks, LAST))
        phik[pair] = phi
        for yk in range(YS):
            m = dot(phi[:, yk * CHUNK : (yk + 1) * CHUNK].astype(BF16), value_one(pair, yk))
            if is_own:
                if yk < YS - 1:
                    state_all[yk] = m
                state_own[yk] = jnp.zeros_like(m)
            else:
                if yk < YS - 1:
                    state_all[yk] += m
                state_own[yk] += jnp.where(pair < zh, m, 0.0)

    def student_own():
        for yq in range(YS):
            q = query(yq)
            pq = jnp.exp(dot(q, w))
            phiq[yq] = pq
            phiqt[yq] = jnp.exp(dot(wt, q, LAST))
            pk = phik[zh, :, yq * CHUNK : (yq + 1) * CHUNK]
            scores = jnp.where(causal, dot3(split(pq), split(pk)), 0.0)
            intra[yq] = dot2(split(scores), value_one(zh, yq))

    def work(pair, is_own):
        teacher(pair, is_own)
        student_keys(pair, is_own)

    for i in (1, 2, 3):
        d = step_of[i]
        ref = at(z, rows[i], c)
        remote(ref, ref, col_send.at[d], col_recv.at[d], device(rows[i], z, c)).wait_recv()
        ring(1, i)
    sibling(0, 0)
    for i in range(YS):
        arrived(1, i)
        ring(2, i)
    sibling(1, 7)
    sibling(2, 1)
    copy_q.wait()
    for dy in (1, 3, 2, 0):
        for dc in (0, 1):
            if dy == 0 and dc == 0:
                continue
            j = dy * 2 + dc
            ref = qbuf.at[other_y(4 - dy), other_c(dc)]
            remote(ref, ref, q_send.at[j], q_recv.at[j], device(other_y(4 - dy), z, other_c(dc))).wait_recv()
    from_sibling(0, 0)
    from_sibling(1, 7)
    from_sibling(2, 1)
    near = lax.rem(zh + 2 * g + 3, 4)
    far = lax.rem(zh + 5 - 2 * g, 4)
    opposite = lax.rem(zh + 2, 4)
    work(zh, True)
    for i in range(YS):
        arrived(2, i)
        ring(3, i)
    sibling(3, 6)
    sibling(4, 2)
    student_own()
    from_sibling(3, 6)
    from_sibling(4, 2)
    work(near, False)
    for i in range(YS):
        arrived(3, i)
        ring(4, i)
    sibling(5, 5)
    sibling(6, 3)
    from_sibling(5, 5)
    from_sibling(6, 3)
    work(far, False)
    for i in range(YS):
        arrived(4, i)
    sibling(7, 4)
    from_sibling(7, 4)
    work(opposite, False)

    grad = jnp.zeros((D, D), F32)
    before = None
    for yq in range(YS):
        state = state_own[yq] if before is None else before + state_own[yq]
        if yq < YS - 1:
            before = state_all[yq] if before is None else before + state_all[yq]
        state = state.astype(BF16)
        nd = intra[yq] + dot(phiq[yq].astype(BF16), state)
        inverse = 1.0 / nd[:, D:]
        student = nd[:, :D] * inverse
        total = jnp.sum(denom[yq], axis=1, keepdims=True)
        target = (numer[yq] / total).astype(BF16).astype(F32)
        dn = (student - target) * (2.0 / tokens) * inverse
        dnd = jnp.concatenate([dn, -dn * student], axis=1)
        dnd2 = split(dnd)
        q = query(yq)
        pqt = phiqt[yq]
        pqt2 = split(pqt)
        cot[yq] = dot(pqt2[0], dnd2[0])
        ds = jnp.where(causal, dot2(dnd2, value_one(zh, yq), LAST), 0.0)
        ds2 = split(ds)
        pk2 = split(phik[zh, :, yq * CHUNK : (yq + 1) * CHUNK])
        dpq = dot3(pk2, ds2, LAST) + dot(state, dnd2[0], LAST)
        dphik_own[yq] = dot3(pqt2, ds2)
        grad = grad + dot2(split(pqt * dpq), q)

    for pair, is_own in ((zh, True), (near, False), (far, False), (opposite, False)):
        after = None
        for yk in reversed(range(YS)):
            if is_own:
                gk = after
            else:
                mine = jnp.where(pair < zh, cot[yk], 0.0)
                gk = mine if after is None else after + mine
            after = cot[yk] if after is None else after + cot[yk]
            if gk is None:
                dpk = dphik_own[yk]
            else:
                dpk = dot(gk.astype(BF16), value_one(pair, yk), LAST)
                if is_own:
                    dpk = dpk + dphik_own[yk]
            e = phik[pair, :, yk * CHUNK : (yk + 1) * CHUNK] * dpk
            grad = grad + dot2(split(e), key(pair, yk))

    grad = grad.T
    for hh in range(PAIRS):
        for k in range(8):
            f1_out[hh, k * 4 : k * 4 + 4, :] = grad[k * 16 + hh * 4 : k * 16 + hh * 4 + 4, :]
    for d in (1, 2, 3):
        hh = lax.rem(zh + d, 4)
        send(f1_out.at[hh], f1_in.at[d], f1_send.at[d], f1_recv.at[d], device(y, 2 * hh + g, c))
    acc = f1_out[zh]
    for d in (1, 2, 3):
        hh = lax.rem(zh + 4 - d, 4)
        remote(f1_in.at[d], f1_in.at[d], f1_send.at[d], f1_recv.at[d], device(y, 2 * hh + g, c)).wait_recv()
        acc = acc + f1_in[d]
    for k in range(16):
        f2_out[k] = acc[2 * k : 2 * k + 2, :]
    for j, (dy, dg, dc) in enumerate(group):
        yy, zz, cc = other_y(dy), z_pair(dg), other_c(dc)
        to = lax.rem(zz, 2) * 8 + yy * 2 + cc
        send(f2_out.at[to], f2_in.at[head], f2_send.at[j], f2_recv.at[j], device(yy, zz, cc))
    out_ref[head] = f2_out[g * 8 + y * 2 + c]
    for j, (dy, dg, dc) in enumerate(group):
        yy, zz, cc = other_y(4 - dy), z_pair(dg), other_c(dc)
        source = yy * 4 + lax.rem(zz, 2) * 2 + cc
        ref = f2_in.at[source]
        remote(ref, ref, f2_send.at[j], f2_recv.at[j], device(yy, zz, cc)).wait_recv()
        out_ref[source] = f2_in[source]
    for copy in sent:
        copy.wait_send()


def per_device(queries, keys, values, feature_map):
    heads = queries.shape[0]
    tokens = keys.shape[1] * lax.axis_size("seq")
    dma = pltpu.SemaphoreType.DMA
    anywhere = pl.BlockSpec(memory_space=pl.ANY)
    return pl.pallas_call(
        functools.partial(kernel, tokens),
        out_shape=jax.ShapeDtypeStruct((heads, 2, D), F32),
        in_specs=[anywhere] * 4,
        out_specs=pl.BlockSpec(memory_space=pltpu.VMEM),
        scratch_shapes=[
            pltpu.VMEM((YS, CORES, BLOCK, D), BF16),
            pltpu.VMEM((2, PAIRS, YS, CORES, BLOCK, D), BF16),
            pltpu.VMEM((D, D), BF16),
            pltpu.VMEM((PAIRS, D, YS * CHUNK), F32),
            pltpu.VMEM((YS, CHUNK, D), F32),
            pltpu.VMEM((YS, D, CHUNK), F32),
            pltpu.VMEM((YS, CHUNK, 2 * D), F32),
            pltpu.VMEM((YS, CHUNK, D), F32),
            pltpu.VMEM((YS, CHUNK, D), F32),
            pltpu.VMEM((YS - 1, D, 2 * D), F32),
            pltpu.VMEM((YS, D, 2 * D), F32),
            pltpu.VMEM((YS, D, 2 * D), F32),
            pltpu.VMEM((YS, D, CHUNK), F32),
            pltpu.VMEM((PAIRS, 32, D), F32),
            pltpu.VMEM((PAIRS, 32, D), F32),
            pltpu.VMEM((16, 2, D), F32),
            pltpu.VMEM((16, 2, D), F32),
            dma((3,)),
            dma((8,)),
            dma((8,)),
            dma((4,)),
            dma((4,)),
            dma((4, 4)),
            dma((4, 4)),
            dma((4, 4)),
            dma((4, 4)),
            dma((8,)),
            dma((8,)),
            dma((4,)),
            dma((4,)),
            dma((15,)),
            dma((15,)),
        ],
        compiler_params=pltpu.CompilerParams(
            collective_id=0, has_side_effects=True, vmem_limit_bytes=40 * 2**20
        ),
    )(queries, keys, values, feature_map)


def solution(mesh):
    rows = P("head", "seq", None)
    return jax.shard_map(
        per_device, mesh=mesh, in_specs=(rows, rows, rows, P("head", None, None)),
        out_specs=P("head", ("grp", "seq"), None), check_vma=False,
    )
```

```python
import functools
import math

import jax
import jax.numpy as jnp
from jax import lax
from jax.experimental import pallas as pl
from jax.experimental.pallas import tpu as pltpu
from jax.sharding import PartitionSpec as P

MESH = pl.DeviceIdType.MESH
F32 = jnp.float32
BF16 = jnp.bfloat16
BLOCK = 128
CHUNK = 256
D = 128
YS, PAIRS, CORES, GRPS = 4, 4, 2, 2
LAST = (((1,), (1,)), ((), ()))
PLAIN = (((1,), (0,)), ((), ()))


def dot(a, b, dims=PLAIN):
    return lax.dot_general(a, b, dims, preferred_element_type=F32)


def split(x):
    hi = x.astype(BF16)
    return hi, (x - hi.astype(F32)).astype(BF16)


def dot2(a, b, dims=PLAIN):
    return dot(a[0], b, dims) + dot(a[1], b, dims)


def dot3(a, b, dims=PLAIN):
    return dot(a[0], b[0], dims) + (dot(a[0], b[1], dims) + dot(a[1], b[0], dims))


def kernel(
    tokens,
    q_ref,
    k_ref,
    v_ref,
    fm_ref,
    out_ref,
    qbuf,
    kv,
    wbuf,
    phik,
    phiq,
    phiqt,
    intra,
    numer,
    denom,
    state_all,
    state_own,
    cot,
    dphik_own,
    f1_out,
    f1_in,
    f2_out,
    f2_in,
    loc_sem,
    q_send,
    q_recv,
    z_send,
    z_recv,
    up_send,
    up_recv,
    down_send,
    down_recv,
    key_send,
    key_recv,
    value_send,
    value_recv,
    sib_send,
    sib_recv,
    f1_send,
    f1_recv,
    f2_send,
    f2_recv,
):
    g = lax.axis_index("grp")
    s = lax.axis_index("seq")
    y = lax.div(s, 8)
    zh = lax.rem(lax.div(s, 2), 4)
    c = lax.rem(s, 2)
    z = 2 * zh + g
    head = y * 4 + g * 2 + c

    def seq_of(yy, hh, cc):
        return yy * 8 + hh * 2 + cc

    def device(yy, zz, cc):
        return {"grp": lax.rem(zz, 2), "seq": seq_of(yy, lax.div(zz, 2), cc)}

    def remote(src, dst, send, recv, dev):
        return pltpu.make_async_remote_copy(
            src_ref=src, dst_ref=dst, send_sem=send, recv_sem=recv,
            device_id=dev, device_id_type=MESH,
        )

    own_copies = [
        pltpu.make_async_copy(k_ref.at[0], kv.at[0, zh, y, c], loc_sem.at[0]),
        pltpu.make_async_copy(v_ref.at[0], kv.at[1, zh, y, c], loc_sem.at[3]),
    ]
    for copy in own_copies:
        copy.start()
    copy_q = pltpu.make_async_copy(q_ref.at[head], qbuf.at[y, c], loc_sem.at[1])
    copy_q.start()
    copy_w = pltpu.make_async_copy(fm_ref.at[head], wbuf, loc_sem.at[2])
    copy_w.start()

    other_y = lambda d: lax.rem(y + d, 4)
    other_z = lambda d: lax.rem(z + d, 8)
    other_c = lambda d: lax.rem(c + d, 2)
    group = [
        (dy, dg, dc)
        for dy in range(YS) for dg in range(GRPS) for dc in range(CORES)
        if (dy, dg, dc) != (0, 0, 0)
    ]
    z_pair = lambda d: 2 * zh + lax.rem(g + d, 2)
    toward = lambda d: lax.rem(z + 32 + d * (2 * g - 1), 8)

    barrier = pltpu.get_barrier_semaphore()
    partners = [device(other_y(dy), z_pair(dg), other_c(dc)) for dy, dg, dc in group]
    partners += [device(y, other_z(2 * d), c) for d in (1, 2, 3)]
    partners += [device(y, toward(d), c) for d in (1, 3)]
    for dev in partners:
        pl.semaphore_signal(barrier, inc=1, device_id=dev, device_id_type=MESH)
    for copy in own_copies:
        copy.wait()
    pl.semaphore_wait(barrier, len(partners))

    sent = []

    def send(*args):
        copy = remote(*args)
        copy.start()
        sent.append(copy)

    near = lax.rem(zh + 2 * g + 3, 4)
    far = lax.rem(zh + 5 - 2 * g, 4)
    opposite = lax.rem(zh + 2, 4)
    pairs = [zh, near, far, opposite]
    up, down, across = other_y(1), other_y(3), other_y(2)

    def block(p, yy):
        return kv.at[:, pairs[p], yy, c]

    def column(p, cc):
        return kv.at[:, pairs[p], :, cc]

    def wait_for(ref, send_sem, recv_sem, dev):
        remote(ref, ref, send_sem, recv_sem, dev).wait_recv()

    def z_arrived(d):
        source = toward(-2 if d == 2 else d)
        wait_for(block(d, y), z_send.at[d], z_recv.at[d], device(y, source, c))

    def row_out(p):
        send(block(p, y), block(p, y), up_send.at[p], up_recv.at[p], device(up, z, c))
        send(block(p, y), block(p, y), down_send.at[p], down_recv.at[p], device(down, z, c))

    def relay(p):
        wait_for(block(p, down), up_send.at[p], up_recv.at[p], device(down, z, c))
        ref = kv.at[0, pairs[p], down, c]
        send(ref, ref, key_send.at[p], key_recv.at[p], device(up, z, c))
        wait_for(block(p, up), down_send.at[p], down_recv.at[p], device(up, z, c))
        ref = kv.at[1, pairs[p], up, c]
        send(ref, ref, value_send.at[p], value_recv.at[p], device(down, z, c))

    def to_sibling(p):
        wait_for(kv.at[0, pairs[p], across, c], key_send.at[p], key_recv.at[p], device(down, z, c))
        wait_for(kv.at[1, pairs[p], across, c], value_send.at[p], value_recv.at[p], device(up, z, c))
        send(column(p, c), column(p, c), sib_send.at[p], sib_recv.at[p], device(y, z, other_c(1)))

    def from_sibling(p):
        wait_for(column(p, other_c(1)), sib_send.at[p], sib_recv.at[p], device(y, z, other_c(1)))

    row_out(0)
    for d in (1, 2, 3):
        send(block(0, y), block(0, y), z_send.at[d], z_recv.at[d], device(y, toward(d), c))
    for dy in (1, 3, 2, 0):
        for dc in (0, 1):
            if dy == 0 and dc == 0:
                continue
            to_head = other_y(dy) * 4 + g * 2 + other_c(dc)
            j = dy * 2 + dc
            send(
                q_ref.at[to_head], qbuf.at[y, c], q_send.at[j], q_recv.at[j],
                device(other_y(dy), z, other_c(dc)),
            )

    copy_w.wait()
    w = wbuf[...]
    wt = w.astype(F32).T.astype(BF16)
    ones = jnp.ones((CHUNK, D), BF16)
    row_id = lax.broadcasted_iota(jnp.int32, (CHUNK, CHUNK), 0)
    col_id = lax.broadcasted_iota(jnp.int32, (CHUNK, CHUNK), 1)
    causal = col_id <= row_id
    scale = math.log2(math.e) / math.sqrt(D)

    def query(yq):
        return qbuf[yq].reshape(CHUNK, D)

    def key(pair, yk):
        return kv[0, pair, yk].reshape(CHUNK, D)

    def value(pair, yk):
        return kv[1, pair, yk].reshape(CHUNK, D)

    def value_one(pair, yk):
        return jnp.concatenate([value(pair, yk), ones], axis=1)

    def attend(pair, yq, first, count, masked, new):
        n = count * CHUNK
        keys = kv[0, pair, pl.ds(first, count)].reshape(n, D)
        vals = kv[1, pair, pl.ds(first, count)].reshape(n, D)
        p = jnp.exp2(dot(query(yq), keys, LAST) * scale)
        if masked:
            p = jnp.where(causal, p, 0.0)
        part = sum(p[:, k * D : (k + 1) * D] for k in range(n // D))
        out = dot(p.astype(BF16), vals)
        if new:
            denom[yq] = part
            numer[yq] = out
        else:
            denom[yq] += part
            numer[yq] += out

    def teacher(pair, is_own):
        for yq in range(YS):
            if is_own:
                attend(pair, yq, yq, 1, True, True)
            if yq > 0:
                attend(pair, yq, 0, yq, False, False)
        if not is_own:

            @pl.when(pair < zh)
            def _():
                for yq in range(YS):
                    attend(pair, yq, yq, 1, False, False)

    def student_keys(pair, is_own):
        ks = kv[0, pair].reshape(YS * CHUNK, D)
        phi = jnp.exp(dot(wt, ks, LAST))
        phik[pair] = phi
        for yk in range(YS):
            m = dot(phi[:, yk * CHUNK : (yk + 1) * CHUNK].astype(BF16), value_one(pair, yk))
            if is_own:
                if yk < YS - 1:
                    state_all[yk] = m
                state_own[yk] = jnp.zeros_like(m)
            else:
                if yk < YS - 1:
                    state_all[yk] += m
                state_own[yk] += jnp.where(pair < zh, m, 0.0)

    def student_own():
        for yq in range(YS):
            q = query(yq)
            pq = jnp.exp(dot(q, w))
            phiq[yq] = pq
            phiqt[yq] = jnp.exp(dot(wt, q, LAST))
            pk = phik[zh, :, yq * CHUNK : (yq + 1) * CHUNK]
            scores = jnp.where(causal, dot3(split(pq), split(pk)), 0.0)
            intra[yq] = dot2(split(scores), value_one(zh, yq))

    def work(pair, is_own):
        teacher(pair, is_own)
        student_keys(pair, is_own)

    z_arrived(1)
    row_out(1)
    relay(0)
    z_arrived(2)
    row_out(2)
    z_arrived(3)
    row_out(3)
    to_sibling(0)
    relay(1)
    copy_q.wait()
    for dy in (1, 3, 2, 0):
        for dc in (0, 1):
            if dy == 0 and dc == 0:
                continue
            j = dy * 2 + dc
            ref = qbuf.at[other_y(4 - dy), other_c(dc)]
            wait_for(ref, q_send.at[j], q_recv.at[j], device(other_y(4 - dy), z, other_c(dc)))
    from_sibling(0)
    work(zh, True)
    relay(2)
    to_sibling(1)
    student_own()
    from_sibling(1)
    work(near, False)
    relay(3)
    to_sibling(2)
    from_sibling(2)
    work(far, False)
    to_sibling(3)
    from_sibling(3)
    work(opposite, False)

    grad = jnp.zeros((D, D), F32)
    before = None
    for yq in range(YS):
        state = state_own[yq] if before is None else before + state_own[yq]
        if yq < YS - 1:
            before = state_all[yq] if before is None else before + state_all[yq]
        state = state.astype(BF16)
        nd = intra[yq] + dot(phiq[yq].astype(BF16), state)
        inverse = 1.0 / nd[:, D:]
        student = nd[:, :D] * inverse
        total = jnp.sum(denom[yq], axis=1, keepdims=True)
        target = (numer[yq] / total).astype(BF16).astype(F32)
        dn = (student - target) * (2.0 / tokens) * inverse
        dnd = jnp.concatenate([dn, -dn * student], axis=1)
        dnd2 = split(dnd)
        q = query(yq)
        pqt = phiqt[yq]
        pqt2 = split(pqt)
        cot[yq] = dot(pqt2[0], dnd2[0])
        ds = jnp.where(causal, dot2(dnd2, value_one(zh, yq), LAST), 0.0)
        ds2 = split(ds)
        pk2 = split(phik[zh, :, yq * CHUNK : (yq + 1) * CHUNK])
        dpq = dot3(pk2, ds2, LAST) + dot(state, dnd2[0], LAST)
        dphik_own[yq] = dot3(pqt2, ds2)
        grad = grad + dot2(split(pqt * dpq), q)

    for pair, is_own in ((zh, True), (near, False), (far, False), (opposite, False)):
        after = None
        for yk in reversed(range(YS)):
            if is_own:
                gk = after
            else:
                mine = jnp.where(pair < zh, cot[yk], 0.0)
                gk = mine if after is None else after + mine
            after = cot[yk] if after is None else after + cot[yk]
            if gk is None:
                dpk = dphik_own[yk]
            else:
                dpk = dot(gk.astype(BF16), value_one(pair, yk), LAST)
                if is_own:
                    dpk = dpk + dphik_own[yk]
            e = phik[pair, :, yk * CHUNK : (yk + 1) * CHUNK] * dpk
            grad = grad + dot2(split(e), key(pair, yk))

    grad = grad.T
    for hh in range(PAIRS):
        for k in range(8):
            f1_out[hh, k * 4 : k * 4 + 4, :] = grad[k * 16 + hh * 4 : k * 16 + hh * 4 + 4, :]
    for d in (1, 2, 3):
        hh = lax.rem(zh + d, 4)
        send(f1_out.at[hh], f1_in.at[d], f1_send.at[d], f1_recv.at[d], device(y, 2 * hh + g, c))
    acc = f1_out[zh]
    for d in (1, 2, 3):
        hh = lax.rem(zh + 4 - d, 4)
        remote(f1_in.at[d], f1_in.at[d], f1_send.at[d], f1_recv.at[d], device(y, 2 * hh + g, c)).wait_recv()
        acc = acc + f1_in[d]
    for k in range(16):
        f2_out[k] = acc[2 * k : 2 * k + 2, :]
    for j, (dy, dg, dc) in enumerate(group):
        yy, zz, cc = other_y(dy), z_pair(dg), other_c(dc)
        to = lax.rem(zz, 2) * 8 + yy * 2 + cc
        send(f2_out.at[to], f2_in.at[head], f2_send.at[j], f2_recv.at[j], device(yy, zz, cc))
    out_ref[head] = f2_out[g * 8 + y * 2 + c]
    for j, (dy, dg, dc) in enumerate(group):
        yy, zz, cc = other_y(4 - dy), z_pair(dg), other_c(dc)
        source = yy * 4 + lax.rem(zz, 2) * 2 + cc
        ref = f2_in.at[source]
        remote(ref, ref, f2_send.at[j], f2_recv.at[j], device(yy, zz, cc)).wait_recv()
        out_ref[source] = f2_in[source]
    for copy in sent:
        copy.wait_send()


def per_device(queries, keys, values, feature_map):
    heads = queries.shape[0]
    tokens = keys.shape[1] * lax.axis_size("seq")
    dma = pltpu.SemaphoreType.DMA
    anywhere = pl.BlockSpec(memory_space=pl.ANY)
    return pl.pallas_call(
        functools.partial(kernel, tokens),
        out_shape=jax.ShapeDtypeStruct((heads, 2, D), F32),
        in_specs=[anywhere] * 4,
        out_specs=pl.BlockSpec(memory_space=pltpu.VMEM),
        scratch_shapes=[
            pltpu.VMEM((YS, CORES, BLOCK, D), BF16),
            pltpu.VMEM((2, PAIRS, YS, CORES, BLOCK, D), BF16),
            pltpu.VMEM((D, D), BF16),
            pltpu.VMEM((PAIRS, D, YS * CHUNK), F32),
            pltpu.VMEM((YS, CHUNK, D), F32),
            pltpu.VMEM((YS, D, CHUNK), F32),
            pltpu.VMEM((YS, CHUNK, 2 * D), F32),
            pltpu.VMEM((YS, CHUNK, D), F32),
            pltpu.VMEM((YS, CHUNK, D), F32),
            pltpu.VMEM((YS - 1, D, 2 * D), F32),
            pltpu.VMEM((YS, D, 2 * D), F32),
            pltpu.VMEM((YS, D, 2 * D), F32),
            pltpu.VMEM((YS, D, CHUNK), F32),
            pltpu.VMEM((PAIRS, 32, D), F32),
            pltpu.VMEM((PAIRS, 32, D), F32),
            pltpu.VMEM((16, 2, D), F32),
            pltpu.VMEM((16, 2, D), F32),
            dma((4,)),
            dma((8,)),
            dma((8,)),
            dma((4,)),
            dma((4,)),
            dma((4,)),
            dma((4,)),
            dma((4,)),
            dma((4,)),
            dma((4,)),
            dma((4,)),
            dma((4,)),
            dma((4,)),
            dma((4,)),
            dma((4,)),
            dma((4,)),
            dma((4,)),
            dma((15,)),
            dma((15,)),
        ],
        compiler_params=pltpu.CompilerParams(
            collective_id=0, has_side_effects=True, vmem_limit_bytes=64 * 2**20 - 2**15
        ),
    )(queries, keys, values, feature_map)


def solution(mesh):
    rows = P("head", "seq", None)
    return jax.shard_map(
        per_device, mesh=mesh, in_specs=(rows, rows, rows, P("head", None, None)),
        out_specs=P("head", ("grp", "seq"), None), check_vma=False,
    )
```

```python
import functools
import math

import jax
import jax.numpy as jnp
from jax import lax
from jax.experimental import pallas as pl
from jax.experimental.pallas import tpu as pltpu
from jax.sharding import PartitionSpec as P

MESH = pl.DeviceIdType.MESH
F32 = jnp.float32
BF16 = jnp.bfloat16
BLOCK = 128
CHUNK = 256
D = 128
YS, PAIRS, CORES, GRPS = 4, 4, 2, 2
LAST = (((1,), (1,)), ((), ()))
PLAIN = (((1,), (0,)), ((), ()))


def dot(a, b, dims=PLAIN):
    return lax.dot_general(a, b, dims, preferred_element_type=F32)


def split(x):
    hi = x.astype(BF16)
    return hi, (x - hi.astype(F32)).astype(BF16)


def dot2(a, b, dims=PLAIN):
    return dot(a[0], b, dims) + dot(a[1], b, dims)


def dot3(a, b, dims=PLAIN):
    return dot(a[0], b[0], dims) + (dot(a[0], b[1], dims) + dot(a[1], b[0], dims))


def kernel(
    tokens,
    q_ref,
    k_ref,
    v_ref,
    fm_ref,
    out_ref,
    qbuf,
    kv,
    wbuf,
    phik,
    phiq,
    phiqt,
    intra,
    numer,
    denom,
    state_all,
    state_own,
    cot,
    dphik_own,
    f1_out,
    f1_in,
    f2_out,
    f2_in,
    loc_sem,
    q_send,
    q_recv,
    z_send,
    z_recv,
    y_send,
    y_recv,
    near_send,
    near_recv,
    sib_send,
    sib_recv,
    f1_send,
    f1_recv,
    f2_send,
    f2_recv,
):
    g = lax.axis_index("grp")
    s = lax.axis_index("seq")
    y = lax.div(s, 8)
    zh = lax.rem(lax.div(s, 2), 4)
    c = lax.rem(s, 2)
    z = 2 * zh + g
    head = y * 4 + g * 2 + c

    def seq_of(yy, hh, cc):
        return yy * 8 + hh * 2 + cc

    def device(yy, zz, cc):
        return {"grp": lax.rem(zz, 2), "seq": seq_of(yy, lax.div(zz, 2), cc)}

    def remote(src, dst, send, recv, dev):
        return pltpu.make_async_remote_copy(
            src_ref=src, dst_ref=dst, send_sem=send, recv_sem=recv,
            device_id=dev, device_id_type=MESH,
        )

    own_copies = [
        pltpu.make_async_copy(k_ref.at[0], kv.at[0, zh, y, c], loc_sem.at[0]),
        pltpu.make_async_copy(v_ref.at[0], kv.at[1, zh, y, c], loc_sem.at[3]),
    ]
    for copy in own_copies:
        copy.start()
    copy_q = pltpu.make_async_copy(q_ref.at[head], qbuf.at[y, c], loc_sem.at[1])
    copy_q.start()
    copy_w = pltpu.make_async_copy(fm_ref.at[head], wbuf, loc_sem.at[2])
    copy_w.start()

    other_y = lambda d: lax.rem(y + d, 4)
    other_z = lambda d: lax.rem(z + d, 8)
    other_c = lambda d: lax.rem(c + d, 2)
    group = [
        (dy, dg, dc)
        for dy in range(YS) for dg in range(GRPS) for dc in range(CORES)
        if (dy, dg, dc) != (0, 0, 0)
    ]
    z_pair = lambda d: 2 * zh + lax.rem(g + d, 2)
    toward = lambda d: lax.rem(z + 32 + d * (2 * g - 1), 8)

    barrier = pltpu.get_barrier_semaphore()
    partners = [device(other_y(dy), z_pair(dg), other_c(dc)) for dy, dg, dc in group]
    partners += [device(y, other_z(2 * d), c) for d in (1, 2, 3)]
    partners += [device(y, toward(d), c) for d in (1, 3)]
    for dev in partners:
        pl.semaphore_signal(barrier, inc=1, device_id=dev, device_id_type=MESH)
    for copy in own_copies:
        copy.wait()
    pl.semaphore_wait(barrier, len(partners))

    sent = []

    def send(*args):
        copy = remote(*args)
        copy.start()
        sent.append(copy)

    near = lax.rem(zh + 2 * g + 3, 4)
    far = lax.rem(zh + 5 - 2 * g, 4)
    opposite = lax.rem(zh + 2, 4)
    pairs = [zh, near, far, opposite]

    def block(p, yy):
        return kv.at[:, pairs[p], yy, c]

    def wait_for(ref, send_sem, recv_sem, dev):
        remote(ref, ref, send_sem, recv_sem, dev).wait_recv()

    def to_sibling(p, dy):
        ref = block(p, other_y(dy))
        send(ref, ref, sib_send.at[p, dy], sib_recv.at[p, dy], device(y, z, other_c(1)))

    def from_sibling(p):
        for dy in range(YS):
            ref = kv.at[:, pairs[p], other_y(dy), other_c(1)]
            wait_for(ref, sib_send.at[p, dy], sib_recv.at[p, dy], device(y, z, other_c(1)))

    def z_arrived(d):
        source = toward(-2 if d == 2 else d)
        wait_for(block(d, y), z_send.at[d], z_recv.at[d], device(y, source, c))
        to_sibling(d, 0)

    def row_out(p):
        for dy in (1, 3, 2):
            send(block(p, y), block(p, y), y_send.at[p, dy], y_recv.at[p, dy], device(other_y(dy), z, c))

    def rows_in(p):
        for dy in (1, 3, 2):
            ref = block(p, other_y(4 - dy))
            wait_for(ref, y_send.at[p, dy], y_recv.at[p, dy], device(other_y(4 - dy), z, c))
            if p == 0:
                send(ref, ref, near_send.at[4 - dy], near_recv.at[4 - dy], device(y, toward(1), c))
            to_sibling(p, 4 - dy)

    def near_in():
        for dy in (3, 1, 2):
            wait_for(block(1, other_y(dy)), near_send.at[dy], near_recv.at[dy], device(y, toward(1), c))
            to_sibling(1, dy)

    row_out(0)
    for d in (1, 2, 3):
        send(block(0, y), block(0, y), z_send.at[d], z_recv.at[d], device(y, toward(d), c))
    to_sibling(0, 0)
    for dy in (1, 3, 2, 0):
        for dc in (0, 1):
            if dy == 0 and dc == 0:
                continue
            to_head = other_y(dy) * 4 + g * 2 + other_c(dc)
            j = dy * 2 + dc
            send(
                q_ref.at[to_head], qbuf.at[y, c], q_send.at[j], q_recv.at[j],
                device(other_y(dy), z, other_c(dc)),
            )

    copy_w.wait()
    w = wbuf[...]
    wt = w.astype(F32).T.astype(BF16)
    ones = jnp.ones((CHUNK, D), BF16)
    row_id = lax.broadcasted_iota(jnp.int32, (CHUNK, CHUNK), 0)
    col_id = lax.broadcasted_iota(jnp.int32, (CHUNK, CHUNK), 1)
    causal = col_id <= row_id
    scale = math.log2(math.e) / math.sqrt(D)

    def query(yq):
        return qbuf[yq].reshape(CHUNK, D)

    def key(pair, yk):
        return kv[0, pair, yk].reshape(CHUNK, D)

    def value(pair, yk):
        return kv[1, pair, yk].reshape(CHUNK, D)

    def value_one(pair, yk):
        return jnp.concatenate([value(pair, yk), ones], axis=1)

    def attend(pair, yq, first, count, masked, new):
        n = count * CHUNK
        keys = kv[0, pair, pl.ds(first, count)].reshape(n, D)
        vals = kv[1, pair, pl.ds(first, count)].reshape(n, D)
        p = jnp.exp2(dot(query(yq), keys, LAST) * scale)
        if masked:
            p = jnp.where(causal, p, 0.0)
        part = sum(p[:, k * D : (k + 1) * D] for k in range(n // D))
        out = dot(p.astype(BF16), vals)
        if new:
            denom[yq] = part
            numer[yq] = out
        else:
            denom[yq] += part
            numer[yq] += out

    def teacher(pair, is_own):
        for yq in range(YS):
            if is_own:
                attend(pair, yq, yq, 1, True, True)
            if yq > 0:
                attend(pair, yq, 0, yq, False, False)
        if not is_own:

            @pl.when(pair < zh)
            def _():
                for yq in range(YS):
                    attend(pair, yq, yq, 1, False, False)

    def student_keys(pair, is_own):
        ks = kv[0, pair].reshape(YS * CHUNK, D)
        phi = jnp.exp(dot(wt, ks, LAST))
        phik[pair] = phi
        for yk in range(YS):
            m = dot(phi[:, yk * CHUNK : (yk + 1) * CHUNK].astype(BF16), value_one(pair, yk))
            if is_own:
                if yk < YS - 1:
                    state_all[yk] = m
                state_own[yk] = jnp.zeros_like(m)
            else:
                if yk < YS - 1:
                    state_all[yk] += m
                state_own[yk] += jnp.where(pair < zh, m, 0.0)

    def student_own():
        for yq in range(YS):
            q = query(yq)
            pq = jnp.exp(dot(q, w))
            phiq[yq] = pq
            phiqt[yq] = jnp.exp(dot(wt, q, LAST))
            pk = phik[zh, :, yq * CHUNK : (yq + 1) * CHUNK]
            scores = jnp.where(causal, dot3(split(pq), split(pk)), 0.0)
            intra[yq] = dot2(split(scores), value_one(zh, yq))

    def work(pair, is_own):
        teacher(pair, is_own)
        student_keys(pair, is_own)

    z_arrived(1)
    rows_in(0)
    z_arrived(2)
    row_out(2)
    z_arrived(3)
    row_out(3)
    copy_q.wait()
    for dy in (1, 3, 2, 0):
        for dc in (0, 1):
            if dy == 0 and dc == 0:
                continue
            j = dy * 2 + dc
            ref = qbuf.at[other_y(4 - dy), other_c(dc)]
            wait_for(ref, q_send.at[j], q_recv.at[j], device(other_y(4 - dy), z, other_c(dc)))
    from_sibling(0)
    work(zh, True)
    near_in()
    student_own()
    rows_in(2)
    from_sibling(1)
    work(near, False)
    rows_in(3)
    from_sibling(2)
    work(far, False)
    from_sibling(3)
    work(opposite, False)

    grad = jnp.zeros((D, D), F32)
    before = None
    for yq in range(YS):
        state = state_own[yq] if before is None else before + state_own[yq]
        if yq < YS - 1:
            before = state_all[yq] if before is None else before + state_all[yq]
        state = state.astype(BF16)
        nd = intra[yq] + dot(phiq[yq].astype(BF16), state)
        inverse = 1.0 / nd[:, D:]
        student = nd[:, :D] * inverse
        total = jnp.sum(denom[yq], axis=1, keepdims=True)
        target = (numer[yq] / total).astype(BF16).astype(F32)
        dn = (student - target) * (2.0 / tokens) * inverse
        dnd = jnp.concatenate([dn, -dn * student], axis=1)
        dnd2 = split(dnd)
        q = query(yq)
        pqt = phiqt[yq]
        pqt2 = split(pqt)
        cot[yq] = dot(pqt2[0], dnd2[0])
        ds = jnp.where(causal, dot2(dnd2, value_one(zh, yq), LAST), 0.0)
        ds2 = split(ds)
        pk2 = split(phik[zh, :, yq * CHUNK : (yq + 1) * CHUNK])
        dpq = dot3(pk2, ds2, LAST) + dot(state, dnd2[0], LAST)
        dphik_own[yq] = dot3(pqt2, ds2)
        grad = grad + dot2(split(pqt * dpq), q)

    for pair, is_own in ((zh, True), (near, False), (far, False), (opposite, False)):
        after = None
        for yk in reversed(range(YS)):
            if is_own:
                gk = after
            else:
                mine = jnp.where(pair < zh, cot[yk], 0.0)
                gk = mine if after is None else after + mine
            after = cot[yk] if after is None else after + cot[yk]
            if gk is None:
                dpk = dphik_own[yk]
            else:
                dpk = dot(gk.astype(BF16), value_one(pair, yk), LAST)
                if is_own:
                    dpk = dpk + dphik_own[yk]
            e = phik[pair, :, yk * CHUNK : (yk + 1) * CHUNK] * dpk
            grad = grad + dot2(split(e), key(pair, yk))

    grad = grad.T
    for hh in range(PAIRS):
        for k in range(8):
            f1_out[hh, k * 4 : k * 4 + 4, :] = grad[k * 16 + hh * 4 : k * 16 + hh * 4 + 4, :]
    for d in (1, 2, 3):
        hh = lax.rem(zh + d, 4)
        send(f1_out.at[hh], f1_in.at[d], f1_send.at[d], f1_recv.at[d], device(y, 2 * hh + g, c))
    acc = f1_out[zh]
    for d in (1, 2, 3):
        hh = lax.rem(zh + 4 - d, 4)
        remote(f1_in.at[d], f1_in.at[d], f1_send.at[d], f1_recv.at[d], device(y, 2 * hh + g, c)).wait_recv()
        acc = acc + f1_in[d]
    for k in range(16):
        f2_out[k] = acc[2 * k : 2 * k + 2, :]
    for j, (dy, dg, dc) in enumerate(group):
        yy, zz, cc = other_y(dy), z_pair(dg), other_c(dc)
        to = lax.rem(zz, 2) * 8 + yy * 2 + cc
        send(f2_out.at[to], f2_in.at[head], f2_send.at[j], f2_recv.at[j], device(yy, zz, cc))
    out_ref[head] = f2_out[g * 8 + y * 2 + c]
    for j, (dy, dg, dc) in enumerate(group):
        yy, zz, cc = other_y(4 - dy), z_pair(dg), other_c(dc)
        source = yy * 4 + lax.rem(zz, 2) * 2 + cc
        ref = f2_in.at[source]
        remote(ref, ref, f2_send.at[j], f2_recv.at[j], device(yy, zz, cc)).wait_recv()
        out_ref[source] = f2_in[source]
    for copy in sent:
        copy.wait_send()


def per_device(queries, keys, values, feature_map):
    heads = queries.shape[0]
    tokens = keys.shape[1] * lax.axis_size("seq")
    dma = pltpu.SemaphoreType.DMA
    anywhere = pl.BlockSpec(memory_space=pl.ANY)
    return pl.pallas_call(
        functools.partial(kernel, tokens),
        out_shape=jax.ShapeDtypeStruct((heads, 2, D), F32),
        in_specs=[anywhere] * 4,
        out_specs=pl.BlockSpec(memory_space=pltpu.VMEM),
        scratch_shapes=[
            pltpu.VMEM((YS, CORES, BLOCK, D), BF16),
            pltpu.VMEM((2, PAIRS, YS, CORES, BLOCK, D), BF16),
            pltpu.VMEM((D, D), BF16),
            pltpu.VMEM((PAIRS, D, YS * CHUNK), F32),
            pltpu.VMEM((YS, CHUNK, D), F32),
            pltpu.VMEM((YS, D, CHUNK), F32),
            pltpu.VMEM((YS, CHUNK, 2 * D), F32),
            pltpu.VMEM((YS, CHUNK, D), F32),
            pltpu.VMEM((YS, CHUNK, D), F32),
            pltpu.VMEM((YS - 1, D, 2 * D), F32),
            pltpu.VMEM((YS, D, 2 * D), F32),
            pltpu.VMEM((YS, D, 2 * D), F32),
            pltpu.VMEM((YS, D, CHUNK), F32),
            pltpu.VMEM((PAIRS, 32, D), F32),
            pltpu.VMEM((PAIRS, 32, D), F32),
            pltpu.VMEM((16, 2, D), F32),
            pltpu.VMEM((16, 2, D), F32),
            dma((4,)),
            dma((8,)),
            dma((8,)),
            dma((4,)),
            dma((4,)),
            dma((4, 4)),
            dma((4, 4)),
            dma((4,)),
            dma((4,)),
            dma((4, 4)),
            dma((4, 4)),
            dma((4,)),
            dma((4,)),
            dma((15,)),
            dma((15,)),
        ],
        compiler_params=pltpu.CompilerParams(
            collective_id=0, has_side_effects=True, vmem_limit_bytes=64 * 2**20 - 2**15
        ),
    )(queries, keys, values, feature_map)


def solution(mesh):
    rows = P("head", "seq", None)
    return jax.shard_map(
        per_device, mesh=mesh, in_specs=(rows, rows, rows, P("head", None, None)),
        out_specs=P("head", ("grp", "seq"), None), check_vma=False,
    )
```

```python
import functools
import math

import jax
import jax.numpy as jnp
from jax import lax
from jax.experimental import pallas as pl
from jax.experimental.pallas import tpu as pltpu
from jax.sharding import PartitionSpec as P

MESH = pl.DeviceIdType.MESH
F32 = jnp.float32
BF16 = jnp.bfloat16
BLOCK = 128
CHUNK = 256
D = 128
YS, PAIRS, CORES, GRPS = 4, 4, 2, 2
LAST = (((1,), (1,)), ((), ()))
PLAIN = (((1,), (0,)), ((), ()))


def dot(a, b, dims=PLAIN):
    return lax.dot_general(a, b, dims, preferred_element_type=F32)


def split(x):
    hi = x.astype(BF16)
    return hi, (x - hi.astype(F32)).astype(BF16)


def dot2(a, b, dims=PLAIN):
    rows = a[0].shape[0]
    both = dot(jnp.concatenate(a, axis=0), b, dims)
    return both[:rows] + both[rows:]


def dot3(a, b, dims=PLAIN):
    return dot2(a, b[0], dims) + dot(a[0], b[1], dims)


def kernel(
    tokens,
    q_ref,
    k_ref,
    v_ref,
    fm_ref,
    out_ref,
    qbuf,
    kv,
    wbuf,
    phik,
    phiq,
    phiqt,
    intra,
    numer,
    denom,
    state_all,
    state_own,
    f1_out,
    f1_in,
    f2_out,
    f2_in,
    loc_sem,
    q_send,
    q_recv,
    z_send,
    z_recv,
    y_send,
    y_recv,
    near_send,
    near_recv,
    sib_send,
    sib_recv,
    f1_send,
    f1_recv,
    f2_send,
    f2_recv,
):
    g = lax.axis_index("grp")
    s = lax.axis_index("seq")
    y = lax.div(s, 8)
    zh = lax.rem(lax.div(s, 2), 4)
    c = lax.rem(s, 2)
    z = 2 * zh + g
    head = y * 4 + g * 2 + c

    def seq_of(yy, hh, cc):
        return yy * 8 + hh * 2 + cc

    def device(yy, zz, cc):
        return {"grp": lax.rem(zz, 2), "seq": seq_of(yy, lax.div(zz, 2), cc)}

    def remote(src, dst, send, recv, dev):
        return pltpu.make_async_remote_copy(
            src_ref=src, dst_ref=dst, send_sem=send, recv_sem=recv,
            device_id=dev, device_id_type=MESH,
        )

    own_copies = [
        pltpu.make_async_copy(k_ref.at[0], kv.at[0, zh, y, c], loc_sem.at[0]),
        pltpu.make_async_copy(v_ref.at[0], kv.at[1, zh, y, c], loc_sem.at[3]),
    ]
    for copy in own_copies:
        copy.start()
    copy_q = pltpu.make_async_copy(q_ref.at[head], qbuf.at[y, c], loc_sem.at[1])
    copy_q.start()
    copy_w = pltpu.make_async_copy(fm_ref.at[head], wbuf, loc_sem.at[2])
    copy_w.start()

    other_y = lambda d: lax.rem(y + d, 4)
    other_z = lambda d: lax.rem(z + d, 8)
    other_c = lambda d: lax.rem(c + d, 2)
    group = [
        (dy, dg, dc)
        for dy in range(YS) for dg in range(GRPS) for dc in range(CORES)
        if (dy, dg, dc) != (0, 0, 0)
    ]
    z_pair = lambda d: 2 * zh + lax.rem(g + d, 2)
    toward = lambda d: lax.rem(z + 32 + d * (2 * g - 1), 8)

    barrier = pltpu.get_barrier_semaphore()
    partners = [device(other_y(dy), z_pair(dg), other_c(dc)) for dy, dg, dc in group]
    partners += [device(y, other_z(2 * d), c) for d in (1, 2, 3)]
    partners += [device(y, toward(d), c) for d in (1, 3)]
    for dev in partners:
        pl.semaphore_signal(barrier, inc=1, device_id=dev, device_id_type=MESH)
    for copy in own_copies:
        copy.wait()
    pl.semaphore_wait(barrier, len(partners))

    sent = []

    def send(*args):
        copy = remote(*args)
        copy.start()
        sent.append(copy)

    near = lax.rem(zh + 2 * g + 3, 4)
    far = lax.rem(zh + 5 - 2 * g, 4)
    opposite = lax.rem(zh + 2, 4)
    pairs = [zh, near, far, opposite]

    def block(p, yy):
        return kv.at[:, pairs[p], yy, c]

    def wait_for(ref, send_sem, recv_sem, dev):
        remote(ref, ref, send_sem, recv_sem, dev).wait_recv()

    def to_sibling(p, dy):
        ref = block(p, other_y(dy))
        send(ref, ref, sib_send.at[p, dy], sib_recv.at[p, dy], device(y, z, other_c(1)))

    def from_sibling(p):
        for dy in range(YS):
            ref = kv.at[:, pairs[p], other_y(dy), other_c(1)]
            wait_for(ref, sib_send.at[p, dy], sib_recv.at[p, dy], device(y, z, other_c(1)))

    def z_arrived(d):
        source = toward(-2 if d == 2 else d)
        wait_for(block(d, y), z_send.at[d], z_recv.at[d], device(y, source, c))
        to_sibling(d, 0)

    def row_out(p):
        for dy in (1, 3, 2):
            send(block(p, y), block(p, y), y_send.at[p, dy], y_recv.at[p, dy], device(other_y(dy), z, c))

    def rows_in(p):
        for dy in (1, 3, 2):
            ref = block(p, other_y(4 - dy))
            wait_for(ref, y_send.at[p, dy], y_recv.at[p, dy], device(other_y(4 - dy), z, c))
            if p == 0:
                send(ref, ref, near_send.at[4 - dy], near_recv.at[4 - dy], device(y, toward(1), c))
            to_sibling(p, 4 - dy)

    def near_in():
        for dy in (3, 1, 2):
            wait_for(block(1, other_y(dy)), near_send.at[dy], near_recv.at[dy], device(y, toward(1), c))
            to_sibling(1, dy)

    row_out(0)
    for d in (1, 2, 3):
        send(block(0, y), block(0, y), z_send.at[d], z_recv.at[d], device(y, toward(d), c))
    to_sibling(0, 0)
    for dy in (1, 3, 2, 0):
        for dc in (0, 1):
            if dy == 0 and dc == 0:
                continue
            to_head = other_y(dy) * 4 + g * 2 + other_c(dc)
            j = dy * 2 + dc
            send(
                q_ref.at[to_head], qbuf.at[y, c], q_send.at[j], q_recv.at[j],
                device(other_y(dy), z, other_c(dc)),
            )

    copy_w.wait()
    w = wbuf[...]
    wt = w.astype(F32).T.astype(BF16)
    ones = jnp.ones((CHUNK, D), BF16)
    row_id = lax.broadcasted_iota(jnp.int32, (CHUNK, CHUNK), 0)
    col_id = lax.broadcasted_iota(jnp.int32, (CHUNK, CHUNK), 1)
    causal = col_id <= row_id
    scale = math.log2(math.e) / math.sqrt(D)

    def query(yq):
        return qbuf[yq].reshape(CHUNK, D)

    def key(pair, yk):
        return kv[0, pair, yk].reshape(CHUNK, D)

    def value(pair, yk):
        return kv[1, pair, yk].reshape(CHUNK, D)

    def value_one(pair, yk):
        return jnp.concatenate([value(pair, yk), ones], axis=1)

    def teacher(pair, is_own):
        for yq in range(YS):
            n = (yq + 1) * CHUNK
            keys = kv[0, pair, 0 : yq + 1].reshape(n, D)
            vals = kv[1, pair, 0 : yq + 1].reshape(n, D)
            p = jnp.exp2(dot(query(yq), keys, LAST) * scale)
            last = jnp.where(causal if is_own else pair < zh, p[:, n - CHUNK :], 0.0)
            p = jnp.concatenate([p[:, : n - CHUNK], last], axis=1) if yq else last
            part = sum(p[:, k * D : (k + 1) * D] for k in range(n // D))
            out = dot(p.astype(BF16), vals)
            if is_own:
                denom[yq] = part
                numer[yq] = out
            else:
                denom[yq] += part
                numer[yq] += out

    def student_keys(pair, is_own):
        ks = kv[0, pair].reshape(YS * CHUNK, D)
        phi = jnp.exp(dot(wt, ks, LAST))
        phik[pair] = phi
        for yk in range(YS):
            m = dot(phi[:, yk * CHUNK : (yk + 1) * CHUNK].astype(BF16), value_one(pair, yk))
            if is_own:
                if yk < YS - 1:
                    state_all[yk] = m
                state_own[yk] = jnp.zeros_like(m)
            else:
                if yk < YS - 1:
                    state_all[yk] += m
                state_own[yk] += jnp.where(pair < zh, m, 0.0)

    def student_own():
        for yq in range(YS):
            q = query(yq)
            pq = jnp.exp(dot(q, w))
            phiq[yq] = pq
            phiqt[yq] = jnp.exp(dot(wt, q, LAST))
            pk = phik[zh, :, yq * CHUNK : (yq + 1) * CHUNK]
            scores = jnp.where(causal, dot3(split(pq), split(pk)), 0.0)
            intra[yq] = dot2(split(scores), value_one(zh, yq))

    def work(pair, is_own):
        teacher(pair, is_own)
        student_keys(pair, is_own)

    z_arrived(1)
    rows_in(0)
    z_arrived(2)
    row_out(2)
    z_arrived(3)
    row_out(3)
    copy_q.wait()
    for dy in (1, 3, 2, 0):
        for dc in (0, 1):
            if dy == 0 and dc == 0:
                continue
            j = dy * 2 + dc
            ref = qbuf.at[other_y(4 - dy), other_c(dc)]
            wait_for(ref, q_send.at[j], q_recv.at[j], device(other_y(4 - dy), z, other_c(dc)))
    from_sibling(0)
    work(zh, True)
    near_in()
    student_own()
    rows_in(2)
    from_sibling(1)
    work(near, False)
    rows_in(3)
    from_sibling(2)
    work(far, False)
    from_sibling(3)
    work(opposite, False)

    chunks = range(YS)
    qs = [query(yq) for yq in chunks]
    vones = [value_one(zh, yq) for yq in chunks]
    states, before = [], None
    for yq in chunks:
        state = state_own[yq] if before is None else before + state_own[yq]
        if yq < YS - 1:
            before = state_all[yq] if before is None else before + state_all[yq]
        states.append(state.astype(BF16))
    outs = [intra[yq] + dot(phiq[yq].astype(BF16), states[yq]) for yq in chunks]
    dnds = []
    for yq in chunks:
        inverse = 1.0 / outs[yq][:, D:]
        student = outs[yq][:, :D] * inverse
        total = jnp.sum(denom[yq], axis=1, keepdims=True)
        target = (numer[yq] / total).astype(BF16).astype(F32)
        dn = (student - target) * (2.0 / tokens) * inverse
        dnds.append(split(jnp.concatenate([dn, -dn * student], axis=1)))
    pqts = [split(phiqt[yq]) for yq in chunks]
    pks = [split(phik[zh, :, yq * CHUNK : (yq + 1) * CHUNK]) for yq in chunks]
    cots = [dot(pqts[yq][0], dnds[yq][0]) for yq in chunks]
    dss = [
        split(jnp.where(causal, dot2(dnds[yq], vones[yq], LAST), 0.0)) for yq in chunks
    ]
    dpqs = [dot3(pks[yq], dss[yq], LAST) + dot(states[yq], dnds[yq][0], LAST) for yq in chunks]
    dpks_own = [dot3(pqts[yq], dss[yq]) for yq in chunks]
    later = [None] * YS
    for yk in reversed(range(YS - 1)):
        later[yk] = cots[yk + 1] if later[yk + 1] is None else later[yk + 1] + cots[yk + 1]
    grad = jnp.zeros((D, D), F32)
    for pair, is_own in ((near, False), (far, False), (opposite, False), (zh, True)):
        dpks = []
        for yk in chunks:
            gk = later[yk]
            if not is_own:
                mine = jnp.where(pair < zh, cots[yk], 0.0)
                gk = mine if gk is None else gk + mine
            dpk = dpks_own[yk] if is_own else None
            if gk is not None:
                far_part = dot(gk.astype(BF16), value_one(pair, yk), LAST)
                dpk = far_part if dpk is None else dpk + far_part
            dpks.append(dpk)
        e = phik[pair] * jnp.concatenate(dpks, axis=1)
        grad = grad + dot2(split(e), kv[0, pair].reshape(YS * CHUNK, D))
    e = jnp.concatenate([phiqt[yq] * dpqs[yq] for yq in chunks], axis=1)
    grad = grad + dot2(split(e), qbuf[...].reshape(YS * CHUNK, D))

    grad = grad.T
    for hh in range(PAIRS):
        for k in range(8):
            f1_out[hh, k * 4 : k * 4 + 4, :] = grad[k * 16 + hh * 4 : k * 16 + hh * 4 + 4, :]
    for d in (1, 2, 3):
        hh = lax.rem(zh + d, 4)
        send(f1_out.at[hh], f1_in.at[d], f1_send.at[d], f1_recv.at[d], device(y, 2 * hh + g, c))
    acc = f1_out[zh]
    for d in (1, 2, 3):
        hh = lax.rem(zh + 4 - d, 4)
        remote(f1_in.at[d], f1_in.at[d], f1_send.at[d], f1_recv.at[d], device(y, 2 * hh + g, c)).wait_recv()
        acc = acc + f1_in[d]
    for k in range(16):
        f2_out[k] = acc[2 * k : 2 * k + 2, :]
    for j, (dy, dg, dc) in enumerate(group):
        yy, zz, cc = other_y(dy), z_pair(dg), other_c(dc)
        to = lax.rem(zz, 2) * 8 + yy * 2 + cc
        send(f2_out.at[to], f2_in.at[head], f2_send.at[j], f2_recv.at[j], device(yy, zz, cc))
    out_ref[head] = f2_out[g * 8 + y * 2 + c]
    for j, (dy, dg, dc) in enumerate(group):
        yy, zz, cc = other_y(4 - dy), z_pair(dg), other_c(dc)
        source = yy * 4 + lax.rem(zz, 2) * 2 + cc
        ref = f2_in.at[source]
        remote(ref, ref, f2_send.at[j], f2_recv.at[j], device(yy, zz, cc)).wait_recv()
        out_ref[source] = f2_in[source]
    for copy in sent:
        copy.wait_send()


def per_device(queries, keys, values, feature_map):
    heads = queries.shape[0]
    tokens = keys.shape[1] * lax.axis_size("seq")
    dma = pltpu.SemaphoreType.DMA
    anywhere = pl.BlockSpec(memory_space=pl.ANY)
    return pl.pallas_call(
        functools.partial(kernel, tokens),
        out_shape=jax.ShapeDtypeStruct((heads, 2, D), F32),
        in_specs=[anywhere] * 4,
        out_specs=pl.BlockSpec(memory_space=pltpu.VMEM),
        scratch_shapes=[
            pltpu.VMEM((YS, CORES, BLOCK, D), BF16),
            pltpu.VMEM((2, PAIRS, YS, CORES, BLOCK, D), BF16),
            pltpu.VMEM((D, D), BF16),
            pltpu.VMEM((PAIRS, D, YS * CHUNK), F32),
            pltpu.VMEM((YS, CHUNK, D), F32),
            pltpu.VMEM((YS, D, CHUNK), F32),
            pltpu.VMEM((YS, CHUNK, 2 * D), F32),
            pltpu.VMEM((YS, CHUNK, D), F32),
            pltpu.VMEM((YS, CHUNK, D), F32),
            pltpu.VMEM((YS - 1, D, 2 * D), F32),
            pltpu.VMEM((YS, D, 2 * D), F32),
            pltpu.VMEM((PAIRS, 32, D), F32),
            pltpu.VMEM((PAIRS, 32, D), F32),
            pltpu.VMEM((16, 2, D), F32),
            pltpu.VMEM((16, 2, D), F32),
            dma((4,)),
            dma((8,)),
            dma((8,)),
            dma((4,)),
            dma((4,)),
            dma((4, 4)),
            dma((4, 4)),
            dma((4,)),
            dma((4,)),
            dma((4, 4)),
            dma((4, 4)),
            dma((4,)),
            dma((4,)),
            dma((15,)),
            dma((15,)),
        ],
        compiler_params=pltpu.CompilerParams(
            collective_id=0, has_side_effects=True, vmem_limit_bytes=64 * 2**20 - 2**15
        ),
    )(queries, keys, values, feature_map)


def solution(mesh):
    rows = P("head", "seq", None)
    return jax.shard_map(
        per_device, mesh=mesh, in_specs=(rows, rows, rows, P("head", None, None)),
        out_specs=P("head", ("grp", "seq"), None), check_vma=False,
    )
```

```python
import functools
import math

import jax
import jax.numpy as jnp
from jax import lax
from jax.experimental import pallas as pl
from jax.experimental.pallas import tpu as pltpu
from jax.sharding import PartitionSpec as P

MESH = pl.DeviceIdType.MESH
F32 = jnp.float32
BF16 = jnp.bfloat16
BLOCK = 128
CHUNK = 256
D = 128
YS, PAIRS, CORES, GRPS = 4, 4, 2, 2
LAST = (((1,), (1,)), ((), ()))
PLAIN = (((1,), (0,)), ((), ()))


def dot(a, b, dims=PLAIN):
    return lax.dot_general(a, b, dims, preferred_element_type=F32)


def split(x):
    hi = x.astype(BF16)
    return hi, (x - hi.astype(F32)).astype(BF16)


def dot2(a, b, dims=PLAIN):
    rows = a[0].shape[0]
    both = dot(jnp.concatenate(a, axis=0), b, dims)
    return both[:rows] + both[rows:]


def dot3(a, b, dims=PLAIN):
    return dot2(a, b[0], dims) + dot(a[0], b[1], dims)


def kernel(
    tokens,
    q_ref,
    k_ref,
    v_ref,
    fm_ref,
    out_ref,
    qbuf,
    kv,
    wbuf,
    phik,
    phiq,
    phiqt,
    intra,
    numer,
    denom,
    state_all,
    state_own,
    f1_out,
    f1_in,
    f2_out,
    f2_in,
    loc_sem,
    q_send,
    q_recv,
    z_send,
    z_recv,
    y_send,
    y_recv,
    near_send,
    near_recv,
    sib_send,
    sib_recv,
    f1_send,
    f1_recv,
    f2_send,
    f2_recv,
):
    g = lax.axis_index("grp")
    s = lax.axis_index("seq")
    y = lax.div(s, 8)
    zh = lax.rem(lax.div(s, 2), 4)
    c = lax.rem(s, 2)
    z = 2 * zh + g
    head = y * 4 + g * 2 + c

    def seq_of(yy, hh, cc):
        return yy * 8 + hh * 2 + cc

    def device(yy, zz, cc):
        return {"grp": lax.rem(zz, 2), "seq": seq_of(yy, lax.div(zz, 2), cc)}

    def remote(src, dst, send, recv, dev):
        return pltpu.make_async_remote_copy(
            src_ref=src, dst_ref=dst, send_sem=send, recv_sem=recv,
            device_id=dev, device_id_type=MESH,
        )

    own_copies = [
        pltpu.make_async_copy(k_ref.at[0], kv.at[0, zh, y, c], loc_sem.at[0]),
        pltpu.make_async_copy(v_ref.at[0], kv.at[1, zh, y, c], loc_sem.at[3]),
    ]
    for copy in own_copies:
        copy.start()
    copy_q = pltpu.make_async_copy(q_ref.at[head], qbuf.at[y, c], loc_sem.at[1])
    copy_q.start()
    copy_w = pltpu.make_async_copy(fm_ref.at[head], wbuf, loc_sem.at[2])
    copy_w.start()

    other_y = lambda d: lax.rem(y + d, 4)
    other_c = lambda d: lax.rem(c + d, 2)
    group = [
        (dy, dg, dc)
        for dy in range(YS) for dg in range(GRPS) for dc in range(CORES)
        if (dy, dg, dc) != (0, 0, 0)
    ]
    z_pair = lambda d: 2 * zh + lax.rem(g + d, 2)
    toward = lambda d: lax.rem(z + 32 + d * (2 * g - 1), 8)

    barrier = pltpu.get_barrier_semaphore()
    partners = [device(y, toward(d), c) for d in (3, 2, 1, -2)]
    partners += [device(other_y(dy), z, other_c(dc)) for dy, dg, dc in group if dg == 0]
    for dev in partners:
        pl.semaphore_signal(barrier, inc=1, device_id=dev, device_id_type=MESH)
    for copy in own_copies:
        copy.wait()
    pl.semaphore_wait(barrier, len(partners))

    sent = []

    def send(*args):
        copy = remote(*args)
        copy.start()
        sent.append(copy)

    near = lax.rem(zh + 2 * g + 3, 4)
    far = lax.rem(zh + 5 - 2 * g, 4)
    opposite = lax.rem(zh + 2, 4)
    pairs = [zh, near, far, opposite]

    def block(p, yy):
        return kv.at[:, pairs[p], yy, c]

    def wait_for(ref, send_sem, recv_sem, dev):
        remote(ref, ref, send_sem, recv_sem, dev).wait_recv()

    def to_sibling(p, dy):
        ref = block(p, other_y(dy))
        send(ref, ref, sib_send.at[p, dy], sib_recv.at[p, dy], device(y, z, other_c(1)))

    def from_sibling(p):
        for dy in range(YS):
            ref = kv.at[:, pairs[p], other_y(dy), other_c(1)]
            wait_for(ref, sib_send.at[p, dy], sib_recv.at[p, dy], device(y, z, other_c(1)))

    def z_arrived(d):
        source = toward(-2 if d == 2 else d)
        wait_for(block(d, y), z_send.at[d], z_recv.at[d], device(y, source, c))
        to_sibling(d, 0)

    def row_out(p):
        for dy in (1, 3, 2):
            send(block(p, y), block(p, y), y_send.at[p, dy], y_recv.at[p, dy], device(other_y(dy), z, c))

    def rows_in(p):
        for dy in (1, 3, 2):
            ref = block(p, other_y(4 - dy))
            wait_for(ref, y_send.at[p, dy], y_recv.at[p, dy], device(other_y(4 - dy), z, c))
            if p == 0:
                send(ref, ref, near_send.at[4 - dy], near_recv.at[4 - dy], device(y, toward(1), c))
            to_sibling(p, 4 - dy)

    def near_in():
        for dy in (3, 1, 2):
            wait_for(block(1, other_y(dy)), near_send.at[dy], near_recv.at[dy], device(y, toward(1), c))
            to_sibling(1, dy)

    row_out(0)
    for d in (1, 2, 3):
        send(block(0, y), block(0, y), z_send.at[d], z_recv.at[d], device(y, toward(d), c))
    to_sibling(0, 0)
    for dy in (1, 3, 2, 0):
        for dc in (0, 1):
            if dy == 0 and dc == 0:
                continue
            to_head = other_y(dy) * 4 + g * 2 + other_c(dc)
            j = dy * 2 + dc
            send(
                q_ref.at[to_head], qbuf.at[y, c], q_send.at[j], q_recv.at[j],
                device(other_y(dy), z, other_c(dc)),
            )

    copy_w.wait()
    w = wbuf[...]
    wt = w.astype(F32).T.astype(BF16)
    ones = jnp.ones((CHUNK, D), BF16)
    row_id = lax.broadcasted_iota(jnp.int32, (CHUNK, CHUNK), 0)
    col_id = lax.broadcasted_iota(jnp.int32, (CHUNK, CHUNK), 1)
    causal = col_id <= row_id
    scale = math.log2(math.e) / math.sqrt(D)

    def query(yq):
        return qbuf[yq].reshape(CHUNK, D)

    def key(pair, yk):
        return kv[0, pair, yk].reshape(CHUNK, D)

    def value(pair, yk):
        return kv[1, pair, yk].reshape(CHUNK, D)

    def value_one(pair, yk):
        return jnp.concatenate([value(pair, yk), ones], axis=1)

    def teacher(pair, is_own):
        for yk in range(YS):
            queries = qbuf[yk:].reshape((YS - yk) * CHUNK, D)
            p = jnp.exp2(dot(queries, key(pair, yk), LAST) * scale)
            first = jnp.where(causal if is_own else pair < zh, p[:CHUNK], 0.0)
            p = jnp.concatenate([first, p[CHUNK:]], axis=0) if yk < YS - 1 else first
            part = p[:, :D] + p[:, D:]
            out = dot(p.astype(BF16), value(pair, yk))
            rows = pl.ds(yk * CHUNK, (YS - yk) * CHUNK)
            if is_own and yk == 0:
                denom[rows] = part
                numer[rows] = out
            else:
                denom[rows] += part
                numer[rows] += out

    def student_keys(pair, is_own):
        ks = kv[0, pair].reshape(YS * CHUNK, D)
        phi = jnp.exp(dot(wt, ks, LAST))
        phik[pair] = phi
        for yk in range(YS):
            m = dot(phi[:, yk * CHUNK : (yk + 1) * CHUNK].astype(BF16), value_one(pair, yk))
            if is_own:
                if yk < YS - 1:
                    state_all[yk] = m
                state_own[yk] = jnp.zeros_like(m)
            else:
                if yk < YS - 1:
                    state_all[yk] += m
                state_own[yk] += jnp.where(pair < zh, m, 0.0)

    def student_own():
        for yq in range(YS):
            q = query(yq)
            pq = jnp.exp(dot(q, w))
            phiq[yq] = pq
            phiqt[yq] = jnp.exp(dot(wt, q, LAST))
            pk = phik[zh, :, yq * CHUNK : (yq + 1) * CHUNK]
            scores = jnp.where(causal, dot3(split(pq), split(pk)), 0.0)
            intra[yq] = dot2(split(scores), value_one(zh, yq))

    def work(pair, is_own):
        teacher(pair, is_own)
        student_keys(pair, is_own)

    z_arrived(1)
    rows_in(0)
    z_arrived(2)
    row_out(2)
    z_arrived(3)
    row_out(3)
    copy_q.wait()
    for dy in (1, 3, 2, 0):
        for dc in (0, 1):
            if dy == 0 and dc == 0:
                continue
            j = dy * 2 + dc
            ref = qbuf.at[other_y(4 - dy), other_c(dc)]
            wait_for(ref, q_send.at[j], q_recv.at[j], device(other_y(4 - dy), z, other_c(dc)))
    from_sibling(0)
    work(zh, True)
    near_in()
    student_own()
    rows_in(2)
    from_sibling(1)
    work(near, False)
    rows_in(3)
    from_sibling(2)
    work(far, False)
    from_sibling(3)
    work(opposite, False)

    chunks = range(YS)
    qs = [query(yq) for yq in chunks]
    vones = [value_one(zh, yq) for yq in chunks]
    states, before = [], None
    for yq in chunks:
        state = state_own[yq] if before is None else before + state_own[yq]
        if yq < YS - 1:
            before = state_all[yq] if before is None else before + state_all[yq]
        states.append(state.astype(BF16))
    outs = [intra[yq] + dot(phiq[yq].astype(BF16), states[yq]) for yq in chunks]
    dnds = []
    for yq in chunks:
        inverse = 1.0 / outs[yq][:, D:]
        student = outs[yq][:, :D] * inverse
        rows = pl.ds(yq * CHUNK, CHUNK)
        total = jnp.sum(denom[rows], axis=1, keepdims=True)
        target = (numer[rows] / total).astype(BF16).astype(F32)
        dn = (student - target) * (2.0 / tokens) * inverse
        dnds.append(split(jnp.concatenate([dn, -dn * student], axis=1)))
    pqts = [split(phiqt[yq]) for yq in chunks]
    pks = [split(phik[zh, :, yq * CHUNK : (yq + 1) * CHUNK]) for yq in chunks]
    cots = [dot(pqts[yq][0], dnds[yq][0]) for yq in chunks]
    dss = [
        split(jnp.where(causal, dot2(dnds[yq], vones[yq], LAST), 0.0)) for yq in chunks
    ]
    dpqs = [dot3(pks[yq], dss[yq], LAST) + dot(states[yq], dnds[yq][0], LAST) for yq in chunks]
    dpks_own = [dot3(pqts[yq], dss[yq]) for yq in chunks]
    later = [None] * YS
    for yk in reversed(range(YS - 1)):
        later[yk] = cots[yk + 1] if later[yk + 1] is None else later[yk + 1] + cots[yk + 1]
    grad = jnp.zeros((D, D), F32)
    for pair, is_own in ((near, False), (far, False), (opposite, False), (zh, True)):
        dpks = []
        for yk in chunks:
            gk = later[yk]
            if not is_own:
                mine = jnp.where(pair < zh, cots[yk], 0.0)
                gk = mine if gk is None else gk + mine
            dpk = dpks_own[yk] if is_own else None
            if gk is not None:
                far_part = dot(gk.astype(BF16), value_one(pair, yk), LAST)
                dpk = far_part if dpk is None else dpk + far_part
            dpks.append(dpk)
        e = phik[pair] * jnp.concatenate(dpks, axis=1)
        grad = grad + dot2(split(e), kv[0, pair].reshape(YS * CHUNK, D))
    e = jnp.concatenate([phiqt[yq] * dpqs[yq] for yq in chunks], axis=1)
    grad = grad + dot2(split(e), qbuf[...].reshape(YS * CHUNK, D))

    grad = grad.T
    for hh in range(PAIRS):
        for k in range(8):
            f1_out[hh, k * 4 : k * 4 + 4, :] = grad[k * 16 + hh * 4 : k * 16 + hh * 4 + 4, :]
    for d in (2, 1, 3):
        hh = lax.rem(zh + d, 4)
        send(f1_out.at[hh], f1_in.at[d], f1_send.at[d], f1_recv.at[d], device(y, 2 * hh + g, c))
    acc = f1_out[zh]
    for d in (1, 2, 3):
        hh = lax.rem(zh + 4 - d, 4)
        remote(f1_in.at[d], f1_in.at[d], f1_send.at[d], f1_recv.at[d], device(y, 2 * hh + g, c)).wait_recv()
        acc = acc + f1_in[d]
    for k in range(16):
        f2_out[k] = acc[2 * k : 2 * k + 2, :]
    for j, (dy, dg, dc) in enumerate(group):
        yy, zz, cc = other_y(dy), z_pair(dg), other_c(dc)
        to = lax.rem(zz, 2) * 8 + yy * 2 + cc
        send(f2_out.at[to], f2_in.at[head], f2_send.at[j], f2_recv.at[j], device(yy, zz, cc))
    out_ref[head] = f2_out[g * 8 + y * 2 + c]
    for j, (dy, dg, dc) in enumerate(group):
        yy, zz, cc = other_y(4 - dy), z_pair(dg), other_c(dc)
        source = yy * 4 + lax.rem(zz, 2) * 2 + cc
        ref = f2_in.at[source]
        remote(ref, ref, f2_send.at[j], f2_recv.at[j], device(yy, zz, cc)).wait_recv()
        out_ref[source] = f2_in[source]
    for copy in sent:
        copy.wait_send()


def per_device(queries, keys, values, feature_map):
    heads = queries.shape[0]
    tokens = keys.shape[1] * lax.axis_size("seq")
    dma = pltpu.SemaphoreType.DMA
    anywhere = pl.BlockSpec(memory_space=pl.ANY)
    return pl.pallas_call(
        functools.partial(kernel, tokens),
        out_shape=jax.ShapeDtypeStruct((heads, 2, D), F32),
        in_specs=[anywhere] * 4,
        out_specs=pl.BlockSpec(memory_space=pltpu.VMEM),
        scratch_shapes=[
            pltpu.VMEM((YS, CORES, BLOCK, D), BF16),
            pltpu.VMEM((2, PAIRS, YS, CORES, BLOCK, D), BF16),
            pltpu.VMEM((D, D), BF16),
            pltpu.VMEM((PAIRS, D, YS * CHUNK), F32),
            pltpu.VMEM((YS, CHUNK, D), F32),
            pltpu.VMEM((YS, D, CHUNK), F32),
            pltpu.VMEM((YS, CHUNK, 2 * D), F32),
            pltpu.VMEM((YS * CHUNK, D), F32),
            pltpu.VMEM((YS * CHUNK, D), F32),
            pltpu.VMEM((YS - 1, D, 2 * D), F32),
            pltpu.VMEM((YS, D, 2 * D), F32),
            pltpu.VMEM((PAIRS, 32, D), F32),
            pltpu.VMEM((PAIRS, 32, D), F32),
            pltpu.VMEM((16, 2, D), F32),
            pltpu.VMEM((16, 2, D), F32),
            dma((4,)),
            dma((8,)),
            dma((8,)),
            dma((4,)),
            dma((4,)),
            dma((4, 4)),
            dma((4, 4)),
            dma((4,)),
            dma((4,)),
            dma((4, 4)),
            dma((4, 4)),
            dma((4,)),
            dma((4,)),
            dma((15,)),
            dma((15,)),
        ],
        compiler_params=pltpu.CompilerParams(
            collective_id=0, has_side_effects=True, vmem_limit_bytes=64 * 2**20 - 2**15
        ),
    )(queries, keys, values, feature_map)


def solution(mesh):
    rows = P("head", "seq", None)
    return jax.shard_map(
        per_device, mesh=mesh, in_specs=(rows, rows, rows, P("head", None, None)),
        out_specs=P("head", ("grp", "seq"), None), check_vma=False,
    )
```

```python
import functools
import math

import jax
import jax.numpy as jnp
from jax import lax
from jax.experimental import pallas as pl
from jax.experimental.pallas import tpu as pltpu
from jax.sharding import PartitionSpec as P

MESH = pl.DeviceIdType.MESH
F32 = jnp.float32
BF16 = jnp.bfloat16
BLOCK = 128
CHUNK = 256
D = 128
YS, PAIRS, CORES, GRPS = 4, 4, 2, 2
LAST = (((1,), (1,)), ((), ()))
PLAIN = (((1,), (0,)), ((), ()))


def dot(a, b, dims=PLAIN):
    return lax.dot_general(a, b, dims, preferred_element_type=F32)


def split(x):
    hi = x.astype(BF16)
    return hi, (x - hi.astype(F32)).astype(BF16)


def dot2(a, b, dims=PLAIN):
    rows = a[0].shape[0]
    both = dot(jnp.concatenate(a, axis=0), b, dims)
    return both[:rows] + both[rows:]


def dot3(a, b, dims=PLAIN):
    return dot2(a, b[0], dims) + dot(a[0], b[1], dims)


def kernel(
    tokens,
    q_ref,
    k_ref,
    v_ref,
    fm_ref,
    out_ref,
    qbuf,
    kv,
    wbuf,
    phik,
    phiq,
    phiqt,
    intra,
    numer,
    denom,
    state_all,
    state_own,
    f1_out,
    f1_in,
    f2_out,
    f2_in,
    loc_sem,
    q_send,
    q_recv,
    z_send,
    z_recv,
    y_send,
    y_recv,
    near_send,
    near_recv,
    sib_send,
    sib_recv,
    f1_send,
    f1_recv,
    f2_send,
    f2_recv,
):
    g = lax.axis_index("grp")
    s = lax.axis_index("seq")
    y = lax.div(s, 8)
    zh = lax.rem(lax.div(s, 2), 4)
    c = lax.rem(s, 2)
    z = 2 * zh + g
    head = y * 4 + g * 2 + c

    def seq_of(yy, hh, cc):
        return yy * 8 + hh * 2 + cc

    def device(yy, zz, cc):
        return {"grp": lax.rem(zz, 2), "seq": seq_of(yy, lax.div(zz, 2), cc)}

    def remote(src, dst, send, recv, dev):
        return pltpu.make_async_remote_copy(
            src_ref=src, dst_ref=dst, send_sem=send, recv_sem=recv,
            device_id=dev, device_id_type=MESH,
        )

    own_copies = [
        pltpu.make_async_copy(k_ref.at[0], kv.at[0, zh, y, c], loc_sem.at[0]),
        pltpu.make_async_copy(v_ref.at[0], kv.at[1, zh, y, c], loc_sem.at[3]),
    ]
    for copy in own_copies:
        copy.start()
    copy_q = pltpu.make_async_copy(q_ref.at[head], qbuf.at[y, c], loc_sem.at[1])
    copy_q.start()
    copy_w = pltpu.make_async_copy(fm_ref.at[head], wbuf, loc_sem.at[2])
    copy_w.start()

    other_y = lambda d: lax.rem(y + d, 4)
    other_c = lambda d: lax.rem(c + d, 2)
    group = [
        (dy, dg, dc)
        for dy in range(YS) for dg in range(GRPS) for dc in range(CORES)
        if (dy, dg, dc) != (0, 0, 0)
    ]
    z_pair = lambda d: 2 * zh + lax.rem(g + d, 2)
    toward = lambda d: lax.rem(z + 32 + d * (2 * g - 1), 8)

    barrier = pltpu.get_barrier_semaphore()
    partners = [device(y, toward(d), c) for d in (3, 2, 1, -2)]
    partners += [device(other_y(dy), z, other_c(dc)) for dy, dg, dc in group if dg == 0]
    for dev in partners:
        pl.semaphore_signal(barrier, inc=1, device_id=dev, device_id_type=MESH)
    for copy in own_copies:
        copy.wait()
    pl.semaphore_wait(barrier, len(partners))

    sent = []

    def send(*args):
        copy = remote(*args)
        copy.start()
        sent.append(copy)

    def settle(count):
        for copy in sent[:count]:
            copy.wait_send()
        del sent[:count]

    near = lax.rem(zh + 2 * g + 3, 4)
    far = lax.rem(zh + 5 - 2 * g, 4)
    opposite = lax.rem(zh + 2, 4)
    pairs = [zh, near, far, opposite]

    def block(p, yy):
        return kv.at[:, pairs[p], yy, c]

    def wait_for(ref, send_sem, recv_sem, dev):
        remote(ref, ref, send_sem, recv_sem, dev).wait_recv()

    def to_sibling(p, dy):
        ref = block(p, other_y(dy))
        send(ref, ref, sib_send.at[p, dy], sib_recv.at[p, dy], device(y, z, other_c(1)))

    def from_sibling(p):
        for dy in range(YS):
            ref = kv.at[:, pairs[p], other_y(dy), other_c(1)]
            wait_for(ref, sib_send.at[p, dy], sib_recv.at[p, dy], device(y, z, other_c(1)))

    def z_arrived(d):
        source = toward(-2 if d == 2 else d)
        wait_for(block(d, y), z_send.at[d], z_recv.at[d], device(y, source, c))
        to_sibling(d, 0)

    def row_out(p):
        for dy in (1, 3, 2):
            send(block(p, y), block(p, y), y_send.at[p, dy], y_recv.at[p, dy], device(other_y(dy), z, c))

    def rows_in(p):
        for dy in (1, 3, 2):
            ref = block(p, other_y(4 - dy))
            wait_for(ref, y_send.at[p, dy], y_recv.at[p, dy], device(other_y(4 - dy), z, c))
            if p == 0:
                send(ref, ref, near_send.at[4 - dy], near_recv.at[4 - dy], device(y, toward(1), c))
            to_sibling(p, 4 - dy)

    def near_in():
        for dy in (3, 1, 2):
            wait_for(block(1, other_y(dy)), near_send.at[dy], near_recv.at[dy], device(y, toward(1), c))
            to_sibling(1, dy)

    row_out(0)
    for d in (1, 2, 3):
        send(block(0, y), block(0, y), z_send.at[d], z_recv.at[d], device(y, toward(d), c))
    to_sibling(0, 0)
    for dy in (1, 3, 2, 0):
        for dc in (0, 1):
            if dy == 0 and dc == 0:
                continue
            to_head = other_y(dy) * 4 + g * 2 + other_c(dc)
            j = dy * 2 + dc
            send(
                q_ref.at[to_head], qbuf.at[y, c], q_send.at[j], q_recv.at[j],
                device(other_y(dy), z, other_c(dc)),
            )

    copy_w.wait()
    w = wbuf[...]
    wt = w.astype(F32).T.astype(BF16)
    ones = jnp.ones((CHUNK, D), BF16)
    row_id = lax.broadcasted_iota(jnp.int32, (CHUNK, CHUNK), 0)
    col_id = lax.broadcasted_iota(jnp.int32, (CHUNK, CHUNK), 1)
    causal = col_id <= row_id
    scale = math.log2(math.e) / math.sqrt(D)

    def query(yq):
        return qbuf[yq].reshape(CHUNK, D)

    def key(pair, yk):
        return kv[0, pair, yk].reshape(CHUNK, D)

    def value(pair, yk):
        return kv[1, pair, yk].reshape(CHUNK, D)

    def value_one(pair, yk):
        return jnp.concatenate([value(pair, yk), ones], axis=1)

    def teacher(pair, is_own):
        for yk in range(YS):
            queries = qbuf[yk:].reshape((YS - yk) * CHUNK, D)
            p = jnp.exp2(dot(queries, key(pair, yk), LAST) * scale)
            first = jnp.where(causal if is_own else pair < zh, p[:CHUNK], 0.0)
            p = jnp.concatenate([first, p[CHUNK:]], axis=0) if yk < YS - 1 else first
            part = p[:, :D] + p[:, D:]
            out = dot(p.astype(BF16), value(pair, yk))
            rows = pl.ds(yk * CHUNK, (YS - yk) * CHUNK)
            if is_own and yk == 0:
                denom[rows] = part
                numer[rows] = out
            else:
                denom[rows] += part
                numer[rows] += out

    def student_keys(pair, is_own):
        ks = kv[0, pair].reshape(YS * CHUNK, D)
        phi = jnp.exp(dot(wt, ks, LAST))
        phik[pair] = phi
        for yk in range(YS):
            m = dot(phi[:, yk * CHUNK : (yk + 1) * CHUNK].astype(BF16), value_one(pair, yk))
            if is_own:
                if yk < YS - 1:
                    state_all[yk] = m
                state_own[yk] = jnp.zeros_like(m)
            else:
                if yk < YS - 1:
                    state_all[yk] += m
                state_own[yk] += jnp.where(pair < zh, m, 0.0)

    def student_own():
        for yq in range(YS):
            q = query(yq)
            pq = jnp.exp(dot(q, w))
            phiq[yq] = pq
            phiqt[yq] = jnp.exp(dot(wt, q, LAST))
            pk = phik[zh, :, yq * CHUNK : (yq + 1) * CHUNK]
            scores = jnp.where(causal, dot3(split(pq), split(pk)), 0.0)
            intra[yq] = dot2(split(scores), value_one(zh, yq))

    def work(pair, is_own):
        teacher(pair, is_own)
        student_keys(pair, is_own)

    z_arrived(1)
    rows_in(0)
    z_arrived(2)
    row_out(2)
    z_arrived(3)
    row_out(3)
    copy_q.wait()
    for dy in (1, 3, 2, 0):
        for dc in (0, 1):
            if dy == 0 and dc == 0:
                continue
            j = dy * 2 + dc
            ref = qbuf.at[other_y(4 - dy), other_c(dc)]
            wait_for(ref, q_send.at[j], q_recv.at[j], device(other_y(4 - dy), z, other_c(dc)))
    from_sibling(0)
    work(zh, True)
    near_in()
    student_own()
    rows_in(2)
    from_sibling(1)
    work(near, False)
    rows_in(3)
    from_sibling(2)
    work(far, False)
    from_sibling(3)
    work(opposite, False)

    chunks = range(YS)
    qs = [query(yq) for yq in chunks]
    twice = [jnp.concatenate([value(zh, yq)] * 2, axis=1) for yq in chunks]
    states, before = [], None
    for yq in chunks:
        state = state_own[yq] if before is None else before + state_own[yq]
        if yq < YS - 1:
            before = state_all[yq] if before is None else before + state_all[yq]
        states.append(state.astype(BF16))
    outs = [intra[yq] + dot(phiq[yq].astype(BF16), states[yq]) for yq in chunks]
    dnds, dns, dds = [], [], []
    for yq in chunks:
        inverse = 1.0 / outs[yq][:, D:]
        student = outs[yq][:, :D] * inverse
        rows = pl.ds(yq * CHUNK, CHUNK)
        total = jnp.sum(denom[rows], axis=1, keepdims=True)
        target = (numer[rows] / total).astype(BF16).astype(F32)
        dn = (student - target) * (2.0 / tokens) * inverse
        dd = -dn * student
        dnds.append(jnp.concatenate([dn, dd], axis=1).astype(BF16))
        dns.append(jnp.concatenate(split(dn), axis=1))
        dds.append(jnp.sum(dd, axis=1, keepdims=True))
    pqts = [split(phiqt[yq]) for yq in chunks]
    pks = [split(phik[zh, :, yq * CHUNK : (yq + 1) * CHUNK]) for yq in chunks]
    cots = [dot(pqts[yq][0], dnds[yq]) for yq in chunks]
    dss = [
        split(jnp.where(causal, dot(dns[yq], twice[yq], LAST) + dds[yq], 0.0)) for yq in chunks
    ]
    dpqs = [dot3(pks[yq], dss[yq], LAST) + dot(states[yq], dnds[yq], LAST) for yq in chunks]
    dpks_own = [dot3(pqts[yq], dss[yq]) for yq in chunks]
    cots = [(m[:, :D], jnp.sum(m[:, D:], axis=1, keepdims=True)) for m in cots]
    add = lambda a, b: (a[0] + b[0], a[1] + b[1])
    later = [None] * YS
    for yk in reversed(range(YS - 1)):
        later[yk] = cots[yk + 1] if later[yk + 1] is None else add(later[yk + 1], cots[yk + 1])
    grad = jnp.zeros((D, D), F32)
    for pair, is_own in ((near, False), (far, False), (opposite, False), (zh, True)):
        dpks = []
        for yk in chunks:
            gk = later[yk]
            if not is_own:
                mine = tuple(jnp.where(pair < zh, part, 0.0) for part in cots[yk])
                gk = mine if gk is None else add(gk, mine)
            dpk = dpks_own[yk] if is_own else None
            if gk is not None:
                far_part = dot(gk[0].astype(BF16), value(pair, yk), LAST) + gk[1]
                dpk = far_part if dpk is None else dpk + far_part
            dpks.append(dpk)
        e = phik[pair] * jnp.concatenate(dpks, axis=1)
        grad = grad + dot2(split(e), kv[0, pair].reshape(YS * CHUNK, D))
    e = jnp.concatenate([phiqt[yq] * dpqs[yq] for yq in chunks], axis=1)
    grad = grad + dot2(split(e), qbuf[...].reshape(YS * CHUNK, D))

    grad = grad.T
    for hh in range(PAIRS):
        for k in range(8):
            f1_out[hh, k * 4 : k * 4 + 4, :] = grad[k * 16 + hh * 4 : k * 16 + hh * 4 + 4, :]
    for d in (2, 1, 3):
        hh = lax.rem(zh + d, 4)
        send(f1_out.at[hh], f1_in.at[d], f1_send.at[d], f1_recv.at[d], device(y, 2 * hh + g, c))
    settle(len(sent) - 3)
    acc = f1_out[zh]
    for d in (1, 2, 3):
        hh = lax.rem(zh + 4 - d, 4)
        remote(f1_in.at[d], f1_in.at[d], f1_send.at[d], f1_recv.at[d], device(y, 2 * hh + g, c)).wait_recv()
        acc = acc + f1_in[d]
    for k in range(16):
        f2_out[k] = acc[2 * k : 2 * k + 2, :]
    for j, (dy, dg, dc) in enumerate(group):
        yy, zz, cc = other_y(dy), z_pair(dg), other_c(dc)
        to = lax.rem(zz, 2) * 8 + yy * 2 + cc
        send(f2_out.at[to], f2_in.at[head], f2_send.at[j], f2_recv.at[j], device(yy, zz, cc))
    settle(3)
    out_ref[head] = f2_out[g * 8 + y * 2 + c]
    for j, (dy, dg, dc) in enumerate(group):
        yy, zz, cc = other_y(4 - dy), z_pair(dg), other_c(dc)
        source = yy * 4 + lax.rem(zz, 2) * 2 + cc
        ref = f2_in.at[source]
        remote(ref, ref, f2_send.at[j], f2_recv.at[j], device(yy, zz, cc)).wait_recv()
        out_ref[source] = f2_in[source]
    settle(len(sent))


def per_device(queries, keys, values, feature_map):
    heads = queries.shape[0]
    tokens = keys.shape[1] * lax.axis_size("seq")
    dma = pltpu.SemaphoreType.DMA
    anywhere = pl.BlockSpec(memory_space=pl.ANY)
    return pl.pallas_call(
        functools.partial(kernel, tokens),
        out_shape=jax.ShapeDtypeStruct((heads, 2, D), F32),
        in_specs=[anywhere] * 4,
        out_specs=pl.BlockSpec(memory_space=pltpu.VMEM),
        scratch_shapes=[
            pltpu.VMEM((YS, CORES, BLOCK, D), BF16),
            pltpu.VMEM((2, PAIRS, YS, CORES, BLOCK, D), BF16),
            pltpu.VMEM((D, D), BF16),
            pltpu.VMEM((PAIRS, D, YS * CHUNK), F32),
            pltpu.VMEM((YS, CHUNK, D), F32),
            pltpu.VMEM((YS, D, CHUNK), F32),
            pltpu.VMEM((YS, CHUNK, 2 * D), F32),
            pltpu.VMEM((YS * CHUNK, D), F32),
            pltpu.VMEM((YS * CHUNK, D), F32),
            pltpu.VMEM((YS - 1, D, 2 * D), F32),
            pltpu.VMEM((YS, D, 2 * D), F32),
            pltpu.VMEM((PAIRS, 32, D), F32),
            pltpu.VMEM((PAIRS, 32, D), F32),
            pltpu.VMEM((16, 2, D), F32),
            pltpu.VMEM((16, 2, D), F32),
            dma((4,)),
            dma((8,)),
            dma((8,)),
            dma((4,)),
            dma((4,)),
            dma((4, 4)),
            dma((4, 4)),
            dma((4,)),
            dma((4,)),
            dma((4, 4)),
            dma((4, 4)),
            dma((4,)),
            dma((4,)),
            dma((15,)),
            dma((15,)),
        ],
        compiler_params=pltpu.CompilerParams(
            collective_id=0, has_side_effects=True, vmem_limit_bytes=64 * 2**20 - 2**15
        ),
    )(queries, keys, values, feature_map)


def solution(mesh):
    rows = P("head", "seq", None)
    return jax.shard_map(
        per_device, mesh=mesh, in_specs=(rows, rows, rows, P("head", None, None)),
        out_specs=P("head", ("grp", "seq"), None), check_vma=False,
    )
```

```python
import functools
import math

import jax
import jax.numpy as jnp
from jax import lax
from jax.experimental import pallas as pl
from jax.experimental.pallas import tpu as pltpu
from jax.sharding import PartitionSpec as P

MESH = pl.DeviceIdType.MESH
F32 = jnp.float32
BF16 = jnp.bfloat16
BLOCK = 128
CHUNK = 256
D = 128
YS, PAIRS, CORES = 4, 4, 2
LAST = (((1,), (1,)), ((), ()))
PLAIN = (((1,), (0,)), ((), ()))


def dot(a, b, dims=PLAIN):
    return lax.dot_general(a, b, dims, preferred_element_type=F32)


def split(x):
    hi = x.astype(BF16)
    return hi, (x - hi.astype(F32)).astype(BF16)


def dot2(a, b, dims=PLAIN):
    rows = a[0].shape[0]
    both = dot(jnp.concatenate(a, axis=0), b, dims)
    return both[:rows] + both[rows:]


def dot3(a, b, dims=PLAIN):
    return dot2(a, b[0], dims) + dot(a[0], b[1], dims)


def kernel(
    tokens,
    q_ref,
    k_ref,
    v_ref,
    fm_ref,
    out_ref,
    qbuf,
    kv,
    wbuf,
    phik,
    phiq,
    phiqt,
    intra,
    numer,
    denom,
    state_all,
    state_own,
    f1_out,
    f1_in,
    f2_out,
    f2_in,
    loc_sem,
    q_send,
    q_recv,
    z_send,
    z_recv,
    y_send,
    y_recv,
    near_send,
    near_recv,
    sib_send,
    sib_recv,
    f1_send,
    f1_recv,
    f2_send,
    f2_recv,
):
    g = lax.axis_index("grp")
    s = lax.axis_index("seq")
    y = lax.div(s, 8)
    zh = lax.rem(lax.div(s, 2), 4)
    c = lax.rem(s, 2)
    z = 2 * zh + g
    head = y * 4 + g * 2 + c

    def seq_of(yy, hh, cc):
        return yy * 8 + hh * 2 + cc

    def device(yy, zz, cc):
        return {"grp": lax.rem(zz, 2), "seq": seq_of(yy, lax.div(zz, 2), cc)}

    def remote(src, dst, send, recv, dev):
        return pltpu.make_async_remote_copy(
            src_ref=src, dst_ref=dst, send_sem=send, recv_sem=recv,
            device_id=dev, device_id_type=MESH,
        )

    own_copies = [
        pltpu.make_async_copy(k_ref.at[0], kv.at[0, zh, y, c], loc_sem.at[0]),
        pltpu.make_async_copy(v_ref.at[0], kv.at[1, zh, y, c], loc_sem.at[3]),
    ]
    for copy in own_copies:
        copy.start()
    copy_q = pltpu.make_async_copy(q_ref.at[head], qbuf.at[y, c], loc_sem.at[1])
    copy_q.start()
    copy_w = pltpu.make_async_copy(fm_ref.at[head], wbuf, loc_sem.at[2])
    copy_w.start()

    other_y = lambda d: lax.rem(y + d, 4)
    other_c = lambda d: lax.rem(c + d, 2)
    group = [
        (dy, dg, dc)
        for dy in (2, 1, 3, 0) for dg in (1, 0) for dc in (1, 0)
        if (dy, dg, dc) != (0, 0, 0)
    ]
    z_pair = lambda d: 2 * zh + lax.rem(g + d, 2)
    toward = lambda d: lax.rem(z + 32 + d * (2 * g - 1), 8)

    barrier = pltpu.get_barrier_semaphore()
    partners = [device(y, toward(d), c) for d in (3, 2, 1, -2)]
    partners += [device(other_y(dy), z, other_c(dc)) for dy, dg, dc in group if dg == 0]
    for dev in partners:
        pl.semaphore_signal(barrier, inc=1, device_id=dev, device_id_type=MESH)
    for copy in own_copies:
        copy.wait()
    pl.semaphore_wait(barrier, len(partners))

    sent = []

    def send(*args):
        copy = remote(*args)
        copy.start()
        sent.append(copy)

    def settle(count):
        for copy in sent[:count]:
            copy.wait_send()
        del sent[:count]

    near = lax.rem(zh + 2 * g + 3, 4)
    far = lax.rem(zh + 5 - 2 * g, 4)
    opposite = lax.rem(zh + 2, 4)
    pairs = [zh, near, far, opposite]

    def block(p, yy):
        return kv.at[:, pairs[p], yy, c]

    def wait_for(ref, send_sem, recv_sem, dev):
        remote(ref, ref, send_sem, recv_sem, dev).wait_recv()

    def to_sibling(p, dy):
        ref = block(p, other_y(dy))
        send(ref, ref, sib_send.at[p, dy], sib_recv.at[p, dy], device(y, z, other_c(1)))

    def from_sibling(p):
        for dy in range(YS):
            ref = kv.at[:, pairs[p], other_y(dy), other_c(1)]
            wait_for(ref, sib_send.at[p, dy], sib_recv.at[p, dy], device(y, z, other_c(1)))

    def z_arrived(d):
        source = toward(-2 if d == 2 else d)
        wait_for(block(d, y), z_send.at[d], z_recv.at[d], device(y, source, c))
        to_sibling(d, 0)

    def row_out(p):
        for dy in (1, 3, 2):
            send(block(p, y), block(p, y), y_send.at[p, dy], y_recv.at[p, dy], device(other_y(dy), z, c))

    def rows_in(p):
        for dy in (1, 3, 2):
            ref = block(p, other_y(4 - dy))
            wait_for(ref, y_send.at[p, dy], y_recv.at[p, dy], device(other_y(4 - dy), z, c))
            if p == 0:
                send(ref, ref, near_send.at[4 - dy], near_recv.at[4 - dy], device(y, toward(1), c))
            to_sibling(p, 4 - dy)

    def near_in():
        for dy in (3, 1, 2):
            wait_for(block(1, other_y(dy)), near_send.at[dy], near_recv.at[dy], device(y, toward(1), c))
            to_sibling(1, dy)

    row_out(0)
    for d in (1, 2, 3):
        send(block(0, y), block(0, y), z_send.at[d], z_recv.at[d], device(y, toward(d), c))
    to_sibling(0, 0)
    for dy in (1, 3, 2, 0):
        for dc in (0, 1):
            if dy == 0 and dc == 0:
                continue
            to_head = other_y(dy) * 4 + g * 2 + other_c(dc)
            j = dy * 2 + dc
            send(
                q_ref.at[to_head], qbuf.at[y, c], q_send.at[j], q_recv.at[j],
                device(other_y(dy), z, other_c(dc)),
            )

    copy_w.wait()
    w = wbuf[...]
    wt = w.astype(F32).T.astype(BF16)
    ones = jnp.ones((CHUNK, D), BF16)
    row_id = lax.broadcasted_iota(jnp.int32, (CHUNK, CHUNK), 0)
    col_id = lax.broadcasted_iota(jnp.int32, (CHUNK, CHUNK), 1)
    causal = col_id <= row_id
    scale = math.log2(math.e) / math.sqrt(D)

    def query(yq):
        return qbuf[yq].reshape(CHUNK, D)

    def key(pair, yk):
        return kv[0, pair, yk].reshape(CHUNK, D)

    def value(pair, yk):
        return kv[1, pair, yk].reshape(CHUNK, D)

    def value_one(pair, yk):
        return jnp.concatenate([value(pair, yk), ones], axis=1)

    def teacher(group, is_own):
        for yk in range(YS):
            queries = qbuf[yk:].reshape((YS - yk) * CHUNK, D)
            keys = jnp.concatenate([key(pair, yk) for pair in group], axis=0)
            vals = jnp.concatenate([value(pair, yk) for pair in group], axis=0)
            p = jnp.exp2(dot(queries, keys, LAST) * scale)
            first = [
                jnp.where(causal if is_own else pair < zh, p[:CHUNK, k * CHUNK : (k + 1) * CHUNK], 0.0)
                for k, pair in enumerate(group)
            ]
            first = jnp.concatenate(first, axis=1)
            p = jnp.concatenate([first, p[CHUNK:]], axis=0) if yk < YS - 1 else first
            part = sum(p[:, k * D : (k + 1) * D] for k in range(2 * len(group)))
            out = dot(p.astype(BF16), vals)
            rows = pl.ds(yk * CHUNK, (YS - yk) * CHUNK)
            if is_own and yk == 0:
                denom[rows] = part
                numer[rows] = out
            else:
                denom[rows] += part
                numer[rows] += out

    def student_keys(pair, is_own):
        ks = kv[0, pair].reshape(YS * CHUNK, D)
        phi = jnp.exp(dot(wt, ks, LAST))
        phik[pair] = phi
        for yk in range(YS):
            m = dot(phi[:, yk * CHUNK : (yk + 1) * CHUNK].astype(BF16), value_one(pair, yk))
            if is_own:
                if yk < YS - 1:
                    state_all[yk] = m
                state_own[yk] = jnp.zeros_like(m)
            else:
                if yk < YS - 1:
                    state_all[yk] += m
                state_own[yk] += jnp.where(pair < zh, m, 0.0)

    def student_own():
        for yq in range(YS):
            q = query(yq)
            pq = jnp.exp(dot(q, w))
            phiq[yq] = pq
            phiqt[yq] = jnp.exp(dot(wt, q, LAST))
            pk = phik[zh, :, yq * CHUNK : (yq + 1) * CHUNK]
            scores = jnp.where(causal, dot3(split(pq), split(pk)), 0.0)
            intra[yq] = dot2(split(scores), value_one(zh, yq))

    def work(group, is_own):
        teacher(group, is_own)
        for pair in group:
            student_keys(pair, is_own)

    z_arrived(1)
    rows_in(0)
    z_arrived(2)
    row_out(2)
    z_arrived(3)
    row_out(3)
    copy_q.wait()
    for dy in (1, 3, 2, 0):
        for dc in (0, 1):
            if dy == 0 and dc == 0:
                continue
            j = dy * 2 + dc
            ref = qbuf.at[other_y(4 - dy), other_c(dc)]
            wait_for(ref, q_send.at[j], q_recv.at[j], device(other_y(4 - dy), z, other_c(dc)))
    from_sibling(0)
    work([zh], True)
    near_in()
    student_own()
    rows_in(2)
    from_sibling(1)
    student_keys(near, False)
    rows_in(3)
    from_sibling(2)
    student_keys(far, False)
    from_sibling(3)
    teacher([near, far, opposite], False)
    student_keys(opposite, False)

    chunks = range(YS)
    qs = [query(yq) for yq in chunks]
    twice = [jnp.concatenate([value(zh, yq)] * 2, axis=1) for yq in chunks]
    states, before = [], None
    for yq in chunks:
        state = state_own[yq] if before is None else before + state_own[yq]
        if yq < YS - 1:
            before = state_all[yq] if before is None else before + state_all[yq]
        states.append(state.astype(BF16))
    outs = [intra[yq] + dot(phiq[yq].astype(BF16), states[yq]) for yq in chunks]
    dnds, dns, dds = [], [], []
    for yq in chunks:
        inverse = 1.0 / outs[yq][:, D:]
        student = outs[yq][:, :D] * inverse
        rows = pl.ds(yq * CHUNK, CHUNK)
        total = jnp.sum(denom[rows], axis=1, keepdims=True)
        target = (numer[rows] / total).astype(BF16).astype(F32)
        dn = (student - target) * (2.0 / tokens) * inverse
        dd = -dn * student
        dnds.append(jnp.concatenate([dn, dd], axis=1).astype(BF16))
        dns.append(jnp.concatenate(split(dn), axis=1))
        dds.append(jnp.sum(dd, axis=1, keepdims=True))
    pqts = [split(phiqt[yq]) for yq in chunks]
    pks = [split(phik[zh, :, yq * CHUNK : (yq + 1) * CHUNK]) for yq in chunks]
    cots = [dot(pqts[yq][0], dnds[yq]) for yq in chunks]
    dss = [
        split(jnp.where(causal, dot(dns[yq], twice[yq], LAST) + dds[yq], 0.0)) for yq in chunks
    ]
    dpqs = [dot3(pks[yq], dss[yq], LAST) + dot(states[yq], dnds[yq], LAST) for yq in chunks]
    dpks_own = [dot3(pqts[yq], dss[yq]) for yq in chunks]
    cots = [(m[:, :D], jnp.sum(m[:, D:], axis=1, keepdims=True)) for m in cots]
    add = lambda a, b: (a[0] + b[0], a[1] + b[1])
    later = [None] * YS
    for yk in reversed(range(YS - 1)):
        later[yk] = cots[yk + 1] if later[yk + 1] is None else add(later[yk + 1], cots[yk + 1])
    grad = jnp.zeros((D, D), F32)
    for pair, is_own in ((near, False), (far, False), (opposite, False), (zh, True)):
        dpks = []
        for yk in chunks:
            gk = later[yk]
            if not is_own:
                mine = tuple(jnp.where(pair < zh, part, 0.0) for part in cots[yk])
                gk = mine if gk is None else add(gk, mine)
            dpk = dpks_own[yk] if is_own else None
            if gk is not None:
                far_part = dot(gk[0].astype(BF16), value(pair, yk), LAST) + gk[1]
                dpk = far_part if dpk is None else dpk + far_part
            dpks.append(dpk)
        e = phik[pair] * jnp.concatenate(dpks, axis=1)
        grad = grad + dot2(split(e), kv[0, pair].reshape(YS * CHUNK, D))
    e = jnp.concatenate([phiqt[yq] * dpqs[yq] for yq in chunks], axis=1)
    grad = grad + dot2(split(e), qbuf[...].reshape(YS * CHUNK, D))

    grad = grad.T
    for hh in range(PAIRS):
        for k in range(8):
            f1_out[hh, k * 4 : k * 4 + 4, :] = grad[k * 16 + hh * 4 : k * 16 + hh * 4 + 4, :]
    for d in (2, 1, 3):
        hh = lax.rem(zh + d, 4)
        send(f1_out.at[hh], f1_in.at[d], f1_send.at[d], f1_recv.at[d], device(y, 2 * hh + g, c))
    settle(len(sent) - 3)
    acc = f1_out[zh]
    for d in (1, 2, 3):
        hh = lax.rem(zh + 4 - d, 4)
        remote(f1_in.at[d], f1_in.at[d], f1_send.at[d], f1_recv.at[d], device(y, 2 * hh + g, c)).wait_recv()
        acc = acc + f1_in[d]
    for k in range(16):
        f2_out[k] = acc[2 * k : 2 * k + 2, :]
    for j, (dy, dg, dc) in enumerate(group):
        yy, zz, cc = other_y(dy), z_pair(dg), other_c(dc)
        to = lax.rem(zz, 2) * 8 + yy * 2 + cc
        send(f2_out.at[to], f2_in.at[head], f2_send.at[j], f2_recv.at[j], device(yy, zz, cc))
    settle(3)
    out_ref[head] = f2_out[g * 8 + y * 2 + c]
    for j, (dy, dg, dc) in enumerate(group):
        yy, zz, cc = other_y(4 - dy), z_pair(dg), other_c(dc)
        source = yy * 4 + lax.rem(zz, 2) * 2 + cc
        ref = f2_in.at[source]
        remote(ref, ref, f2_send.at[j], f2_recv.at[j], device(yy, zz, cc)).wait_recv()
        out_ref[source] = f2_in[source]
    settle(len(sent))


def per_device(queries, keys, values, feature_map):
    heads = queries.shape[0]
    tokens = keys.shape[1] * lax.axis_size("seq")
    dma = pltpu.SemaphoreType.DMA
    anywhere = pl.BlockSpec(memory_space=pl.ANY)
    return pl.pallas_call(
        functools.partial(kernel, tokens),
        out_shape=jax.ShapeDtypeStruct((heads, 2, D), F32),
        in_specs=[anywhere] * 4,
        out_specs=pl.BlockSpec(memory_space=pltpu.VMEM),
        scratch_shapes=[
            pltpu.VMEM((YS, CORES, BLOCK, D), BF16),
            pltpu.VMEM((2, PAIRS, YS, CORES, BLOCK, D), BF16),
            pltpu.VMEM((D, D), BF16),
            pltpu.VMEM((PAIRS, D, YS * CHUNK), F32),
            pltpu.VMEM((YS, CHUNK, D), F32),
            pltpu.VMEM((YS, D, CHUNK), F32),
            pltpu.VMEM((YS, CHUNK, 2 * D), F32),
            pltpu.VMEM((YS * CHUNK, D), F32),
            pltpu.VMEM((YS * CHUNK, D), F32),
            pltpu.VMEM((YS - 1, D, 2 * D), F32),
            pltpu.VMEM((YS, D, 2 * D), F32),
            pltpu.VMEM((PAIRS, 32, D), F32),
            pltpu.VMEM((PAIRS, 32, D), F32),
            pltpu.VMEM((16, 2, D), F32),
            pltpu.VMEM((16, 2, D), F32),
            dma((4,)),
            dma((8,)),
            dma((8,)),
            dma((4,)),
            dma((4,)),
            dma((4, 4)),
            dma((4, 4)),
            dma((4,)),
            dma((4,)),
            dma((4, 4)),
            dma((4, 4)),
            dma((4,)),
            dma((4,)),
            dma((15,)),
            dma((15,)),
        ],
        compiler_params=pltpu.CompilerParams(
            collective_id=0, has_side_effects=True, vmem_limit_bytes=64 * 2**20 - 2**15
        ),
    )(queries, keys, values, feature_map)


def solution(mesh):
    rows = P("head", "seq", None)
    return jax.shard_map(
        per_device, mesh=mesh, in_specs=(rows, rows, rows, P("head", None, None)),
        out_specs=P("head", ("grp", "seq"), None), check_vma=False,
    )
```

```python
import functools
import math

import jax
import jax.numpy as jnp
from jax import lax
from jax.experimental import pallas as pl
from jax.experimental.pallas import tpu as pltpu
from jax.sharding import PartitionSpec as P

MESH = pl.DeviceIdType.MESH
F32 = jnp.float32
BF16 = jnp.bfloat16
BLOCK = 128
CHUNK = 256
D = 128
YS, PAIRS, CORES = 4, 4, 2
LAST = (((1,), (1,)), ((), ()))
PLAIN = (((1,), (0,)), ((), ()))


def dot(a, b, dims=PLAIN):
    return lax.dot_general(a, b, dims, preferred_element_type=F32)


def split(x):
    hi = x.astype(BF16)
    return hi, (x - hi.astype(F32)).astype(BF16)


def dot2(a, b, dims=PLAIN):
    rows = a[0].shape[0]
    both = dot(jnp.concatenate(a, axis=0), b, dims)
    return both[:rows] + both[rows:]


def dot3(a, b, dims=PLAIN):
    return dot2(a, b[0], dims) + dot(a[0], b[1], dims)


def kernel(
    tokens,
    q_ref,
    k_ref,
    v_ref,
    fm_ref,
    out_ref,
    qbuf,
    kv,
    wbuf,
    phik,
    phiq,
    phiqt,
    intra,
    numer,
    denom,
    state_all,
    state_own,
    f1_out,
    f1_in,
    f2_out,
    f2_in,
    loc_sem,
    q_send,
    q_recv,
    z_send,
    z_recv,
    y_send,
    y_recv,
    near_send,
    near_recv,
    sib_send,
    sib_recv,
    f1_send,
    f1_recv,
    f2_send,
    f2_recv,
):
    g = lax.axis_index("grp")
    s = lax.axis_index("seq")
    y = lax.div(s, 8)
    zh = lax.rem(lax.div(s, 2), 4)
    c = lax.rem(s, 2)
    z = 2 * zh + g
    head = y * 4 + g * 2 + c

    def seq_of(yy, hh, cc):
        return yy * 8 + hh * 2 + cc

    def device(yy, zz, cc):
        return {"grp": lax.rem(zz, 2), "seq": seq_of(yy, lax.div(zz, 2), cc)}

    def remote(src, dst, send, recv, dev):
        return pltpu.make_async_remote_copy(
            src_ref=src, dst_ref=dst, send_sem=send, recv_sem=recv,
            device_id=dev, device_id_type=MESH,
        )

    own_copies = [
        pltpu.make_async_copy(k_ref.at[0], kv.at[0, zh, y, c], loc_sem.at[0]),
        pltpu.make_async_copy(v_ref.at[0], kv.at[1, zh, y, c], loc_sem.at[3]),
    ]
    for copy in own_copies:
        copy.start()
    copy_q = pltpu.make_async_copy(q_ref.at[head], qbuf.at[y, c], loc_sem.at[1])
    copy_q.start()
    copy_w = pltpu.make_async_copy(fm_ref.at[head], wbuf, loc_sem.at[2])
    copy_w.start()

    other_y = lambda d: lax.rem(y + d, 4)
    other_c = lambda d: lax.rem(c + d, 2)
    group = [
        (dy, dg, dc)
        for dy in (2, 1, 3, 0) for dg in (1, 0) for dc in (1, 0)
        if (dy, dg, dc) != (0, 0, 0)
    ]
    z_pair = lambda d: 2 * zh + lax.rem(g + d, 2)
    toward = lambda d: lax.rem(z + 32 + d * (2 * g - 1), 8)

    barrier = pltpu.get_barrier_semaphore()
    partners = [device(y, toward(d), c) for d in (3, 2, 1, -2)]
    partners += [device(other_y(dy), z, other_c(dc)) for dy, dg, dc in group if dg == 0]
    for dev in partners:
        pl.semaphore_signal(barrier, inc=1, device_id=dev, device_id_type=MESH)
    for copy in own_copies:
        copy.wait()
    pl.semaphore_wait(barrier, len(partners))

    sent = []

    def send(*args):
        copy = remote(*args)
        copy.start()
        sent.append(copy)

    def settle(count):
        for copy in sent[:count]:
            copy.wait_send()
        del sent[:count]

    near = lax.rem(zh + 2 * g + 3, 4)
    far = lax.rem(zh + 5 - 2 * g, 4)
    opposite = lax.rem(zh + 2, 4)
    pairs = [zh, near, far, opposite]

    def block(p, yy):
        return kv.at[:, pairs[p], yy, c]

    def wait_for(ref, send_sem, recv_sem, dev):
        remote(ref, ref, send_sem, recv_sem, dev).wait_recv()

    def to_sibling(p, dy):
        ref = block(p, other_y(dy))
        send(ref, ref, sib_send.at[p, dy], sib_recv.at[p, dy], device(y, z, other_c(1)))

    def from_sibling(p):
        for dy in range(YS):
            ref = kv.at[:, pairs[p], other_y(dy), other_c(1)]
            wait_for(ref, sib_send.at[p, dy], sib_recv.at[p, dy], device(y, z, other_c(1)))

    def z_arrived(d):
        source = toward(-2 if d == 2 else d)
        wait_for(block(d, y), z_send.at[d], z_recv.at[d], device(y, source, c))
        to_sibling(d, 0)

    def row_out(p):
        for dy in (1, 3, 2):
            send(block(p, y), block(p, y), y_send.at[p, dy], y_recv.at[p, dy], device(other_y(dy), z, c))

    def rows_in(p):
        for dy in (1, 3, 2):
            ref = block(p, other_y(4 - dy))
            wait_for(ref, y_send.at[p, dy], y_recv.at[p, dy], device(other_y(4 - dy), z, c))
            if p == 0:
                send(ref, ref, near_send.at[4 - dy], near_recv.at[4 - dy], device(y, toward(1), c))
            to_sibling(p, 4 - dy)

    def near_in():
        for dy in (3, 1, 2):
            wait_for(block(1, other_y(dy)), near_send.at[dy], near_recv.at[dy], device(y, toward(1), c))
            to_sibling(1, dy)

    row_out(0)
    for d in (1, 2, 3):
        send(block(0, y), block(0, y), z_send.at[d], z_recv.at[d], device(y, toward(d), c))
    to_sibling(0, 0)
    for dy in (1, 3, 2, 0):
        for dc in (0, 1):
            if dy == 0 and dc == 0:
                continue
            to_head = other_y(dy) * 4 + g * 2 + other_c(dc)
            j = dy * 2 + dc
            send(
                q_ref.at[to_head], qbuf.at[y, c], q_send.at[j], q_recv.at[j],
                device(other_y(dy), z, other_c(dc)),
            )

    copy_w.wait()
    w = wbuf[...]
    wt = w.astype(F32).T.astype(BF16)
    ones = jnp.ones((CHUNK, D), BF16)
    row_id = lax.broadcasted_iota(jnp.int32, (CHUNK, CHUNK), 0)
    col_id = lax.broadcasted_iota(jnp.int32, (CHUNK, CHUNK), 1)
    causal = col_id <= row_id
    scale = math.log2(math.e) / math.sqrt(D)

    def query(yq):
        return qbuf[yq].reshape(CHUNK, D)

    def key(pair, yk):
        return kv[0, pair, yk].reshape(CHUNK, D)

    def value(pair, yk):
        return kv[1, pair, yk].reshape(CHUNK, D)

    def value_one(pair, yk):
        return jnp.concatenate([value(pair, yk), ones], axis=1)

    def teacher(group, is_own):
        for yk in range(YS):
            queries = qbuf[yk:].reshape((YS - yk) * CHUNK, D)
            keys = jnp.concatenate([key(pair, yk) for pair in group], axis=0)
            vals = jnp.concatenate([value(pair, yk) for pair in group], axis=0)
            p = jnp.exp2(dot(queries, keys, LAST) * scale)
            first = [
                jnp.where(causal if is_own else pair < zh, p[:CHUNK, k * CHUNK : (k + 1) * CHUNK], 0.0)
                for k, pair in enumerate(group)
            ]
            first = jnp.concatenate(first, axis=1)
            p = jnp.concatenate([first, p[CHUNK:]], axis=0) if yk < YS - 1 else first
            part = sum(p[:, k * D : (k + 1) * D] for k in range(2 * len(group)))
            out = dot(p.astype(BF16), vals)
            rows = pl.ds(yk * CHUNK, (YS - yk) * CHUNK)
            if is_own and yk == 0:
                denom[rows] = part
                numer[rows] = out
            else:
                denom[rows] += part
                numer[rows] += out

    def student_keys(pair, is_own):
        ks = kv[0, pair].reshape(YS * CHUNK, D)
        phi = jnp.exp(dot(wt, ks, LAST))
        phik[pair] = phi
        for yk in range(YS):
            m = dot(phi[:, yk * CHUNK : (yk + 1) * CHUNK].astype(BF16), value_one(pair, yk))
            if is_own:
                if yk < YS - 1:
                    state_all[yk] = m
                state_own[yk] = jnp.zeros_like(m)
            else:
                if yk < YS - 1:
                    state_all[yk] += m
                state_own[yk] += jnp.where(pair < zh, m, 0.0)

    def student_own():
        for yq in range(YS):
            q = query(yq)
            pq = jnp.exp(dot(q, w))
            phiq[yq] = pq
            phiqt[yq] = jnp.exp(dot(wt, q, LAST))
            pk = phik[zh, :, yq * CHUNK : (yq + 1) * CHUNK]
            scores = jnp.where(causal, dot3(split(pq), split(pk)), 0.0)
            intra[yq] = dot2(split(scores), value_one(zh, yq))

    def work(group, is_own):
        teacher(group, is_own)
        for pair in group:
            student_keys(pair, is_own)

    z_arrived(1)
    rows_in(0)
    z_arrived(2)
    row_out(2)
    z_arrived(3)
    row_out(3)
    copy_q.wait()
    for dy in (1, 3, 2, 0):
        for dc in (0, 1):
            if dy == 0 and dc == 0:
                continue
            j = dy * 2 + dc
            ref = qbuf.at[other_y(4 - dy), other_c(dc)]
            wait_for(ref, q_send.at[j], q_recv.at[j], device(other_y(4 - dy), z, other_c(dc)))
    from_sibling(0)
    work([zh], True)
    near_in()
    student_own()
    rows_in(2)
    from_sibling(1)
    student_keys(near, False)
    rows_in(3)
    from_sibling(2)
    student_keys(far, False)
    from_sibling(3)
    teacher([near, far, opposite], False)
    student_keys(opposite, False)

    chunks = range(YS)
    qs = [query(yq) for yq in chunks]
    twice = [jnp.concatenate([value(zh, yq)] * 2, axis=1) for yq in chunks]
    states, before = [], None
    for yq in chunks:
        state = state_own[yq] if before is None else before + state_own[yq]
        if yq < YS - 1:
            before = state_all[yq] if before is None else before + state_all[yq]
        states.append(state.astype(BF16))
    outs = [intra[yq] + dot(phiq[yq].astype(BF16), states[yq]) for yq in chunks]
    dnds, dns, dds = [], [], []
    for yq in chunks:
        inverse = 1.0 / outs[yq][:, D:]
        student = outs[yq][:, :D] * inverse
        rows = pl.ds(yq * CHUNK, CHUNK)
        total = jnp.sum(denom[rows], axis=1, keepdims=True)
        target = (numer[rows] / total).astype(BF16).astype(F32)
        dn = (student - target) * (2.0 / tokens) * inverse
        dd = -dn * student
        dnds.append(jnp.concatenate([dn, dd], axis=1).astype(BF16))
        dns.append(jnp.concatenate(split(dn), axis=1))
        dds.append(jnp.sum(dd, axis=1, keepdims=True))
    pqts = [split(phiqt[yq]) for yq in chunks]
    pks = [split(phik[zh, :, yq * CHUNK : (yq + 1) * CHUNK]) for yq in chunks]
    cots = [dot(pqts[yq][0], dnds[yq]) for yq in chunks]
    dss = [
        split(jnp.where(causal, dot(dns[yq], twice[yq], LAST) + dds[yq], 0.0)) for yq in chunks
    ]
    dpqs = [dot3(pks[yq], dss[yq], LAST) + dot(states[yq], dnds[yq], LAST) for yq in chunks]
    dpks_own = [dot3(pqts[yq], dss[yq]) for yq in chunks]
    cots = [(m[:, :D], jnp.sum(m[:, D:], axis=1, keepdims=True)) for m in cots]
    add = lambda a, b: (a[0] + b[0], a[1] + b[1])
    later = [None] * YS
    for yk in reversed(range(YS - 1)):
        later[yk] = cots[yk + 1] if later[yk + 1] is None else add(later[yk + 1], cots[yk + 1])
    grad = jnp.zeros((D, D), F32)
    for pair, is_own in ((near, False), (far, False), (opposite, False), (zh, True)):
        dpks = []
        for yk in chunks:
            gk = later[yk]
            if not is_own:
                mine = tuple(jnp.where(pair < zh, part, 0.0) for part in cots[yk])
                gk = mine if gk is None else add(gk, mine)
            dpk = dpks_own[yk] if is_own else None
            if gk is not None:
                far_part = dot(gk[0].astype(BF16), value(pair, yk), LAST) + gk[1]
                dpk = far_part if dpk is None else dpk + far_part
            dpks.append(dpk)
        e = phik[pair] * jnp.concatenate(dpks, axis=1)
        grad = grad + dot2(split(e), kv[0, pair].reshape(YS * CHUNK, D))
    e = jnp.concatenate([phiqt[yq] * dpqs[yq] for yq in chunks], axis=1)
    grad = grad + dot2(split(e), qbuf[...].reshape(YS * CHUNK, D))

    grad = grad.T
    for hh in range(PAIRS):
        for k in range(8):
            f1_out[hh, k * 4 : k * 4 + 4, :] = grad[k * 16 + hh * 4 : k * 16 + hh * 4 + 4, :]
    for d in (2, 1, 3):
        hh = lax.rem(zh + d, 4)
        send(f1_out.at[hh], f1_in.at[d], f1_send.at[d], f1_recv.at[d], device(y, 2 * hh + g, c))
    settle(len(sent) - 3)
    acc = f1_out[zh]
    for d in (1, 2, 3):
        hh = lax.rem(zh + 4 - d, 4)
        remote(f1_in.at[d], f1_in.at[d], f1_send.at[d], f1_recv.at[d], device(y, 2 * hh + g, c)).wait_recv()
        acc = acc + f1_in[d]
    for k in range(16):
        f2_out[k] = acc[2 * k : 2 * k + 2, :]
    for j, (dy, dg, dc) in enumerate(group):
        yy, zz, cc = other_y(dy), z_pair(dg), other_c(dc)
        to = lax.rem(zz, 2) * 8 + yy * 2 + cc
        send(f2_out.at[to], f2_in.at[head], f2_send.at[j], f2_recv.at[0], device(yy, zz, cc))
    settle(3)
    f2_in[head] = f2_out[g * 8 + y * 2 + c]
    every = f2_in.at[pl.ds(0, len(group))]
    wait_for(every, f2_send.at[0], f2_recv.at[0], partners[-1])
    out_ref[...] = f2_in[...]
    settle(len(sent))


def per_device(queries, keys, values, feature_map):
    heads = queries.shape[0]
    tokens = keys.shape[1] * lax.axis_size("seq")
    dma = pltpu.SemaphoreType.DMA
    anywhere = pl.BlockSpec(memory_space=pl.ANY)
    return pl.pallas_call(
        functools.partial(kernel, tokens),
        out_shape=jax.ShapeDtypeStruct((heads, 2, D), F32),
        in_specs=[anywhere] * 4,
        out_specs=pl.BlockSpec(memory_space=pltpu.VMEM),
        scratch_shapes=[
            pltpu.VMEM((YS, CORES, BLOCK, D), BF16),
            pltpu.VMEM((2, PAIRS, YS, CORES, BLOCK, D), BF16),
            pltpu.VMEM((D, D), BF16),
            pltpu.VMEM((PAIRS, D, YS * CHUNK), F32),
            pltpu.VMEM((YS, CHUNK, D), F32),
            pltpu.VMEM((YS, D, CHUNK), F32),
            pltpu.VMEM((YS, CHUNK, 2 * D), F32),
            pltpu.VMEM((YS * CHUNK, D), F32),
            pltpu.VMEM((YS * CHUNK, D), F32),
            pltpu.VMEM((YS - 1, D, 2 * D), F32),
            pltpu.VMEM((YS, D, 2 * D), F32),
            pltpu.VMEM((PAIRS, 32, D), F32),
            pltpu.VMEM((PAIRS, 32, D), F32),
            pltpu.VMEM((16, 2, D), F32),
            pltpu.VMEM((16, 2, D), F32),
            dma((4,)),
            dma((8,)),
            dma((8,)),
            dma((4,)),
            dma((4,)),
            dma((4, 4)),
            dma((4, 4)),
            dma((4,)),
            dma((4,)),
            dma((4, 4)),
            dma((4, 4)),
            dma((4,)),
            dma((4,)),
            dma((15,)),
            dma((15,)),
        ],
        compiler_params=pltpu.CompilerParams(
            collective_id=0, has_side_effects=True, vmem_limit_bytes=64 * 2**20 - 2**15
        ),
    )(queries, keys, values, feature_map)


def solution(mesh):
    rows = P("head", "seq", None)
    return jax.shard_map(
        per_device, mesh=mesh, in_specs=(rows, rows, rows, P("head", None, None)),
        out_specs=P("head", ("grp", "seq"), None), check_vma=False,
    )
```
